512 devices in a mesh: replica: 64 (over z_hi, y, core), tensor: 8 (over x, z_lo).
Axes of the slice: x: 4, y: 8, z: 8 (z_hi: 4, z_lo: 2; z = z_hi * 2 + z_lo), core: 2. Of those that a mesh axis runs over, the one named last changes fastest.
Arguments:
- weights: bfloat16 [3, 64, 224, 13824], P(None, 'replica', None, 'tensor'), may hold values from -6 to 6
- vectors: float32 [3, 64, 8, 13824], P(None, 'replica', None, 'tensor'), may hold values from -6 to 6
Outputs:
- new_weights: bfloat16 [3, 64, 224, 13824], P(None, 'replica', None, 'tensor')
- new_vectors: float32 [3, 64, 8, 13824], P(None, 'replica', None, 'tensor')
The draws below stay inside these ranges and needn't reach their ends.
All inputs are finite; a program needn't handle non-finite values.
Results may differ from the reference program's by a relative error of at most 0.0049.
Values may be sent and summed in bfloat16 or wider, within the bound.
No kernel may reach another device: no remote copies, remote signals or barrier semaphores. Data moves between devices by JAX's collectives and lax.ppermute only.
A program may use at most 64 MiB of HBM per device.

```python
import jax
import jax.numpy as jnp
from jax import lax

FF = 13824
ROWS = 224
MATS = 3
RANK = 8
REPLICAS = 64


def level_of(own_key, dims, split, smallest, high):
    loudness, own = 1.0, jax.random.fold_in(own_key, 6)
    for position, shards_of in split:
        draws = jnp.exp(jax.random.uniform(jax.random.fold_in(own, position), (shards_of,), jnp.float32, smallest / len(split), high / len(split)))
        loudness = loudness * jnp.repeat(draws, dims[position] // shards_of).reshape([-1 if axis == position else 1 for axis in range(len(dims))])
    return loudness


def noise(rng, dims, width, reach, split=(), kind=jnp.bfloat16):
    factor_of = level_of(rng, dims, split, -0.22, 0.18) if split else 1.0
    result = jax.random.normal(rng, dims, jnp.float32) * width * factor_of
    return jnp.minimum(jnp.maximum(result, -reach), reach).astype(kind)


def setup_inputs(seed: int = 0) -> dict:
    keys = jax.random.split(jax.random.key(seed), 3)
    weights = noise(keys[0], (MATS, REPLICAS, ROWS, FF), 1.0, 6.0, ((1, 64), (3, 8)))
    vectors = noise(keys[1], (MATS, REPLICAS, RANK, FF), 1.0, 6.0, ((1, 64), (3, 8)), jnp.float32)
    return {"weights": weights, "vectors": vectors}


def reference(weights, vectors):
    highest = lax.Precision.HIGHEST
    count = weights.shape[1]
    vectors_b = vectors.astype(jnp.bfloat16).astype(jnp.float32)

    def images(index):
        window = lax.dynamic_index_in_dim(weights, index, 1, keepdims=False).astype(jnp.float32)
        prev_index = (index + count - 1) % count
        own_vec = lax.dynamic_index_in_dim(vectors_b, index, 1, keepdims=False)
        prev_vec = lax.dynamic_index_in_dim(vectors_b, prev_index, 1, keepdims=False)
        own_img = jnp.einsum('mkf,mnf->mkn', own_vec, window, precision=highest)
        prev_img = jnp.einsum('mkf,mnf->mkn', prev_vec, window, precision=highest)
        return (own_img, prev_img)
    own_images, prev_images = lax.map(images, jnp.arange(count, dtype=jnp.int32))
    next_images = jnp.roll(prev_images, -1, axis=0)
    edge_images = own_images - next_images
    gram = jnp.einsum('emkn,emjn->emkj', edge_images, edge_images, precision=highest)
    lower = jnp.linalg.cholesky(gram)
    basis = lax.linalg.triangular_solve(lower, edge_images, left_side=True, lower=True)
    basis_b = lax.optimization_barrier(basis.astype(jnp.bfloat16)).astype(jnp.float32)

    def column_factor(index):
        next_index = (index + 1) % count
        window = lax.dynamic_index_in_dim(weights, index, 1, keepdims=False).astype(jnp.float32)
        window_next = lax.dynamic_index_in_dim(weights, next_index, 1, keepdims=False).astype(jnp.float32)
        edge_basis = lax.dynamic_index_in_dim(basis_b, index, 0, keepdims=False)
        first = jnp.einsum('mkn,mnf->mkf', edge_basis, window, precision=highest)
        second = jnp.einsum('mkn,mnf->mkf', edge_basis, window_next, precision=highest)
        return first - second
    factors = lax.map(column_factor, jnp.arange(count, dtype=jnp.int32))

    def updated(index):
        prev_index = (index + count - 1) % count
        window = lax.dynamic_index_in_dim(weights, index, 1, keepdims=False).astype(jnp.float32)
        basis_own = lax.dynamic_index_in_dim(basis, index, 0, keepdims=False)
        basis_prev = lax.dynamic_index_in_dim(basis, prev_index, 0, keepdims=False)
        factor_own = lax.dynamic_index_in_dim(factors, index, 0, keepdims=False)
        factor_prev = lax.dynamic_index_in_dim(factors, prev_index, 0, keepdims=False)
        correction = jnp.einsum('mkn,mkf->mnf', basis_own, factor_own, precision=highest)
        correction = correction - jnp.einsum('mkn,mkf->mnf', basis_prev, factor_prev, precision=highest)
        return (window - 0.5 * correction).astype(jnp.bfloat16)
    new_weights = lax.map(updated, jnp.arange(count, dtype=jnp.int32))
    return (jnp.transpose(new_weights, (1, 0, 2, 3)), jnp.transpose(factors, (1, 0, 2, 3)))
```

```python
import functools

import jax
import jax.numpy as jnp
from jax import lax
from jax.experimental import pallas as pl
from jax.experimental.pallas import tpu as pltpu
from jax.sharding import PartitionSpec as P

LANES = 128
ROWS_BY_ROWS = (((1,), (1,)), ((), ()))
IN_VMEM = pl.BlockSpec(memory_space=pltpu.VMEM)


def shifted(value, axis, steps):
    count = lax.axis_size(axis)
    pairs = [(source, (source + steps) % count) for source in range(count)]
    return lax.ppermute(value, axis, pairs)


def padded(size):
    return -(-size // LANES) * LANES


def images_of(vectors_ref, window_ref, mat):
    return lax.dot_general(
        vectors_ref[mat].astype(jnp.bfloat16),
        window_ref[mat],
        ROWS_BY_ROWS,
        preferred_element_type=jnp.float32,
    )


def own_images_kernel(vectors_ref, window_ref, images_ref):
    mats, rank, _ = vectors_ref.shape
    for mat in range(mats):
        images_ref[mat * rank : (mat + 1) * rank] = images_of(vectors_ref, window_ref, mat)


def differences_kernel(vectors_ref, images_ref, window_ref, differences_ref):
    mats, rank, _ = vectors_ref.shape
    for mat in range(mats):
        rows = slice(mat * rank, (mat + 1) * rank)
        differences_ref[rows] = images_ref[rows] - images_of(vectors_ref, window_ref, mat)


def orthonormal_rows(gram, images, rank):
    mats = gram.shape[0] // rank
    grams = [gram[mat * rank : (mat + 1) * rank] for mat in range(mats)]
    rows = [images[mat * rank : (mat + 1) * rank] for mat in range(mats)]
    place = lax.broadcasted_iota(jnp.int32, (rank, 1), 0)
    pivots = [jnp.ones((rank, 1), jnp.float32) for _ in range(mats)]
    for step in range(rank):
        for mat in range(mats):
            column = grams[mat][:, mat * rank + step : mat * rank + step + 1]
            pivot = column[step : step + 1]
            pivots[mat] = jnp.where(place == step, pivot, pivots[mat])
            if step < rank - 1:
                factor = jnp.where(place > step, column / pivot, 0.0)
                rows[mat] = rows[mat] - factor * rows[mat][step : step + 1]
                grams[mat] = grams[mat] - factor * grams[mat][step : step + 1]
    return jnp.concatenate([row / jnp.sqrt(pivot) for row, pivot in zip(rows, pivots)], 0)


def column_products(basis, window_ref, mats):
    rank = basis.shape[0] // mats
    return [
        jnp.dot(
            basis[mat * rank : (mat + 1) * rank].astype(jnp.bfloat16),
            window_ref[mat],
            preferred_element_type=jnp.float32,
        )
        for mat in range(mats)
    ]


def basis_kernel(parts_ref, window_ref, message_ref, basis_ref):
    mats, row_count, columns = window_ref.shape
    images = jnp.sum(parts_ref[...], 0)
    gram = lax.dot_general(
        images, images, ROWS_BY_ROWS, precision=lax.Precision.HIGHEST, preferred_element_type=jnp.float32
    )
    basis = orthonormal_rows(gram, images, images.shape[0] // mats)
    basis_ref[...] = basis
    high = basis.astype(jnp.bfloat16)
    low = (basis - high.astype(jnp.float32)).astype(jnp.bfloat16)
    start = padded(columns)
    message_ref[:, start : start + row_count] = high
    start += padded(row_count)
    message_ref[:, start : start + row_count] = low
    products = jnp.concatenate(column_products(basis, window_ref, mats), 0)
    message_ref[:, :columns] = products.astype(jnp.bfloat16)


def factors_kernel(message_ref, window_ref, factors_ref, rounded_ref):
    mats, row_count, columns = window_ref.shape
    start = padded(columns)
    high = message_ref[:, start : start + row_count].astype(jnp.float32)
    products = jnp.concatenate(column_products(high, window_ref, mats), 0)
    factors = products - message_ref[:, :columns].astype(jnp.float32)
    factors_ref[...] = factors
    rounded_ref[...] = factors.astype(jnp.bfloat16)


def split(value):
    high = value.astype(jnp.bfloat16).astype(jnp.float32)
    return high, value - high


def left_kernel(message_ref, basis_ref, left_ref):
    mats, row_count, _ = left_ref.shape
    rank = basis_ref.shape[0] // mats
    start = message_ref.shape[1] - 2 * padded(row_count)
    upper_high = -0.5 * message_ref[:, start : start + row_count].astype(jnp.float32)
    start += padded(row_count)
    upper_low = -0.5 * message_ref[:, start : start + row_count].astype(jnp.float32)
    lower_high, lower_low = split(0.5 * basis_ref[...])
    for mat in range(mats):
        rows = slice(mat * rank, (mat + 1) * rank)
        parts = [upper_high[rows], upper_low[rows], upper_high[rows], lower_high[rows], lower_low[rows]]
        left_ref[mat] = jnp.concatenate(parts, 0).T.astype(jnp.bfloat16)


def update_kernel(left_ref, factors_ref, lower_ref, window_ref, updated_ref, held_ref, sems):
    mats, _, columns = window_ref.shape
    rank = factors_ref.shape[0] // mats
    width = 2 * LANES
    copies = []
    for mat in range(mats):
        rows = slice(mat * rank, (mat + 1) * rank)
        for start in range(0, columns, width):
            stop = min(start + width, columns)
            high, low = split(factors_ref[rows, start:stop])
            lower = lower_ref[:, start:stop].astype(jnp.float32)[rows]
            right = jnp.concatenate([high, high, low, lower, lower], 0).astype(jnp.bfloat16)
            change = jnp.dot(left_ref[mat], right, preferred_element_type=jnp.float32)
            held_ref[mat, :, start:stop] = (
                window_ref[mat, :, start:stop].astype(jnp.float32) + change
            ).astype(jnp.bfloat16)
        copies.append(pltpu.make_async_copy(held_ref.at[mat], updated_ref.at[mat, 0], sems.at[mat]))
        copies[-1].start()
    for copy in copies:
        copy.wait()


def call(kernel, outs, in_count, flops, **more):
    return pl.pallas_call(
        kernel,
        out_shape=outs,
        in_specs=[IN_VMEM] * in_count,
        cost_estimate=pl.CostEstimate(flops=flops, bytes_accessed=1 << 20, transcendentals=0),
        compiler_params=pltpu.CompilerParams(vmem_limit_bytes=24 << 20),
        **more,
    )


def shards(weights, vectors):
    window = weights[:, 0]
    own_vectors = vectors[:, 0]
    mats, rank, columns = own_vectors.shape
    row_count = window.shape[1]
    stacked = mats * rank
    product_flops = 2 * stacked * row_count * columns
    f32, bf16 = jnp.float32, jnp.bfloat16
    shape = jax.ShapeDtypeStruct
    out = IN_VMEM

    left_vectors = shifted(own_vectors, "replica", 1)
    own_images = call(own_images_kernel, shape((stacked, row_count), f32), 2, product_flops, out_specs=out)(
        own_vectors, window
    )
    left_images = shifted(own_images, "replica", 1)
    partial_differences = call(
        differences_kernel, shape((stacked, row_count), f32), 3, product_flops, out_specs=out
    )(left_vectors, left_images, window)
    group = lax.axis_size("tensor")
    parts = lax.all_to_all(
        jnp.broadcast_to(partial_differences[None], (group, stacked, row_count)), "tensor", 0, 0
    )
    message_width = padded(columns) + 2 * padded(row_count)
    message, lower_basis = call(
        basis_kernel,
        (shape((stacked, message_width), bf16), shape((stacked, row_count), f32)),
        2,
        product_flops,
        out_specs=(out, out),
    )(parts, window)
    message = shifted(message, "replica", -1)
    factors, rounded = call(
        factors_kernel,
        (shape((stacked, columns), f32), shape((stacked, columns), bf16)),
        2,
        product_flops,
        out_specs=(out, out),
    )(message, window)
    lower_factors = shifted(rounded, "replica", 1)
    left = call(left_kernel, shape((mats, row_count, 5 * rank), bf16), 2, product_flops // 4, out_specs=out)(
        message, lower_basis
    )
    updated = call(
        update_kernel,
        shape((mats, 1, row_count, columns), bf16),
        4,
        5 * product_flops,
        out_specs=pl.BlockSpec(memory_space=pl.ANY),
        scratch_shapes=[pltpu.VMEM((mats, row_count, columns), bf16), pltpu.SemaphoreType.DMA((mats,))],
    )(left, factors, lower_factors, window)
    return (updated, factors.reshape(mats, 1, rank, columns))


def solution(mesh):
    placed = (P(None, "replica", None, "tensor"), P(None, "replica", None, "tensor"))
    return jax.shard_map(
        shards,
        mesh=mesh,
        in_specs=placed,
        out_specs=(P(None, "replica", None, "tensor"), P(None, "replica", None, "tensor")),
        check_vma=False,
    )
```

```python
import functools

import jax
import jax.numpy as jnp
from jax import lax
from jax.experimental import pallas as pl
from jax.experimental.pallas import tpu as pltpu
from jax.sharding import PartitionSpec as P

LANES = 128
ROWS_BY_ROWS = (((1,), (1,)), ((), ()))
IN_VMEM = pl.BlockSpec(memory_space=pltpu.VMEM)


def shifted(value, axis, steps):
    count = lax.axis_size(axis)
    pairs = [(source, (source + steps) % count) for source in range(count)]
    return lax.ppermute(value, axis, pairs)


def padded(size):
    return -(-size // LANES) * LANES


def images_of(vectors_ref, window_ref, mat):
    return lax.dot_general(
        vectors_ref[mat], window_ref[mat], ROWS_BY_ROWS, preferred_element_type=jnp.float32
    )


def staging_kernel(vectors_hbm, window_hbm, vectors_ref, images_ref, window_ref, held_ref, sems):
    mats, rank, _ = vectors_ref.shape
    vectors_copy = pltpu.make_async_copy(vectors_hbm, held_ref, sems.at[mats])
    vectors_copy.start()
    copies = [
        pltpu.make_async_copy(window_hbm.at[mat], window_ref.at[mat], sems.at[mat]) for mat in range(mats)
    ]
    for copy in copies:
        copy.start()
    vectors_copy.wait()
    vectors_ref[...] = held_ref[...].astype(jnp.bfloat16)
    for mat, copy in enumerate(copies):
        copy.wait()
        images_ref[mat * rank : (mat + 1) * rank] = images_of(vectors_ref, window_ref, mat)


def images_kernel(vectors_ref, window_ref, images_ref):
    mats, rank, _ = vectors_ref.shape
    for mat in range(mats):
        images_ref[mat * rank : (mat + 1) * rank] = images_of(vectors_ref, window_ref, mat)


def orthonormal_rows(gram, images, rank):
    mats = gram.shape[0] // rank
    grams = [gram[mat * rank : (mat + 1) * rank] for mat in range(mats)]
    rows = [images[mat * rank : (mat + 1) * rank] for mat in range(mats)]
    place = lax.broadcasted_iota(jnp.int32, (rank, 1), 0)
    pivots = [jnp.ones((rank, 1), jnp.float32) for _ in range(mats)]
    for step in range(rank):
        for mat in range(mats):
            column = grams[mat][:, mat * rank + step : mat * rank + step + 1]
            pivot = column[step : step + 1]
            pivots[mat] = jnp.where(place == step, pivot, pivots[mat])
            if step < rank - 1:
                factor = jnp.where(place > step, column / pivot, 0.0)
                rows[mat] = rows[mat] - factor * rows[mat][step : step + 1]
                grams[mat] = grams[mat] - factor * grams[mat][step : step + 1]
    return jnp.concatenate([row / jnp.sqrt(pivot) for row, pivot in zip(rows, pivots)], 0)


def split(value):
    high = value.astype(jnp.bfloat16).astype(jnp.float32)
    return high, value - high


def basis_kernel(mats, parts_ref, basis_ref, message_ref):
    rank = parts_ref.shape[1] // mats
    row_count = parts_ref.shape[2]
    images = jnp.sum(parts_ref[...], 0)
    gram = lax.dot_general(
        images, images, ROWS_BY_ROWS, precision=lax.Precision.HIGHEST, preferred_element_type=jnp.float32
    )
    basis = orthonormal_rows(gram, images, rank)
    basis_ref[...] = basis
    high, low = split(basis)
    message_ref[:, :row_count] = high.astype(jnp.bfloat16)
    start = padded(row_count)
    message_ref[:, start : start + row_count] = low.astype(jnp.bfloat16)


def products_kernel(message_ref, window_ref, products_ref, rounded_ref):
    mats, row_count, _ = window_ref.shape
    rank = message_ref.shape[0] // mats
    basis = message_ref[:, :row_count].astype(jnp.float32)
    for mat in range(mats):
        rows = slice(mat * rank, (mat + 1) * rank)
        products_ref[rows] = jnp.dot(
            basis[rows].astype(jnp.bfloat16), window_ref[mat], preferred_element_type=jnp.float32
        )
    rounded_ref[...] = products_ref[...].astype(jnp.bfloat16)


def left_kernel(message_ref, basis_ref, left_ref):
    mats, row_count, _ = left_ref.shape
    rank = basis_ref.shape[0] // mats
    start = padded(row_count)
    upper_high = -0.5 * message_ref[:, :row_count].astype(jnp.float32)
    upper_low = -0.5 * message_ref[:, start : start + row_count].astype(jnp.float32)
    lower_high, lower_low = split(0.5 * basis_ref[...])
    for mat in range(mats):
        rows = slice(mat * rank, (mat + 1) * rank)
        parts = [upper_high[rows], upper_low[rows], upper_high[rows], lower_high[rows], lower_low[rows], lower_high[rows]]
        left_ref[mat] = jnp.concatenate(parts, 0).T.astype(jnp.bfloat16)


def update_kernel(
    left_ref, upper_ref, next_ref, lower_ref, previous_ref, window_ref, updated_ref, factors_ref, held_ref, sums_ref, sems
):
    mats, row_count, columns = window_ref.shape
    rank = upper_ref.shape[0] // mats
    width = 2 * LANES
    pieces = sems.shape[1] - 1
    piece = row_count // pieces
    copies = []
    for mat in range(mats):
        rows = slice(mat * rank, (mat + 1) * rank)
        rights = []
        for start in range(0, columns, width):
            stop = min(start + width, columns)
            upper = upper_ref[rows, start:stop] - next_ref[:, start:stop].astype(jnp.float32)[rows]
            sums_ref[mat, 0, :, start:stop] = upper
            upper_high, upper_low = split(upper)
            lower = previous_ref[:, start:stop].astype(jnp.float32)[rows] - lower_ref[rows, start:stop]
            lower_high, lower_low = split(lower)
            parts = [upper_high, upper_high, upper_low, lower_high, lower_high, lower_low]
            rights.append((start, stop, jnp.concatenate(parts, 0).astype(jnp.bfloat16)))
        copies.append(pltpu.make_async_copy(sums_ref.at[mat], factors_ref.at[mat], sems.at[mat, pieces]))
        copies[-1].start()
        for index in range(pieces):
            own = slice(index * piece, (index + 1) * piece)
            left = left_ref[mat, own]
            for start, stop, right in rights:
                change = jnp.dot(left, right, preferred_element_type=jnp.float32)
                held_ref[mat, own, start:stop] = (
                    window_ref[mat, own, start:stop].astype(jnp.float32) + change
                ).astype(jnp.bfloat16)
            copies.append(
                pltpu.make_async_copy(held_ref.at[mat, own], updated_ref.at[mat, 0, own], sems.at[mat, index])
            )
            copies[-1].start()
    for copy in copies:
        copy.wait()


def call(kernel, outs, flops, in_specs=None, out_specs=None, **more):
    def run(*operands):
        return pl.pallas_call(
            kernel,
            out_shape=outs,
            in_specs=[IN_VMEM] * len(operands) if in_specs is None else in_specs,
            out_specs=jax.tree.map(lambda _: IN_VMEM, outs) if out_specs is None else out_specs,
            cost_estimate=pl.CostEstimate(flops=flops, bytes_accessed=1 << 20, transcendentals=0),
            compiler_params=pltpu.CompilerParams(vmem_limit_bytes=24 << 20),
            **more,
        )(*operands)

    return run


def shards(weights, vectors):
    window = weights[:, 0]
    own_vectors = vectors[:, 0]
    mats, rank, columns = own_vectors.shape
    row_count = window.shape[1]
    stacked = mats * rank
    flops = 2 * stacked * row_count * columns

    def whole(dtype, *dims):
        return jax.ShapeDtypeStruct(dims, dtype)

    f32, bf16 = jnp.float32, jnp.bfloat16
    images = whole(f32, stacked, row_count)
    rounded_images = whole(bf16, stacked, row_count)
    products = whole(f32, stacked, columns)
    rounded_products = whole(bf16, stacked, columns)

    vectors_b, own_images, window = call(
        staging_kernel,
        (whole(bf16, *own_vectors.shape), images, whole(bf16, *window.shape)),
        flops,
        in_specs=[pl.BlockSpec(memory_space=pltpu.HBM)] * 2,
        scratch_shapes=[pltpu.VMEM(own_vectors.shape, f32), pltpu.SemaphoreType.DMA((mats + 1,))],
    )(*(pltpu.with_memory_space_constraint(value, pltpu.HBM) for value in (own_vectors, window)))
    left_vectors = shifted(vectors_b, "replica", 1)
    left_images = shifted(own_images, "replica", 1)
    next_images = call(images_kernel, images, flops)(left_vectors, window)
    group = lax.axis_size("tensor")
    parts = lax.all_to_all(
        jnp.broadcast_to((left_images - next_images)[None], (group, stacked, row_count)), "tensor", 0, 0
    )
    lower_basis, message = call(
        functools.partial(basis_kernel, mats),
        (images, whole(bf16, stacked, padded(row_count) + row_count)),
        flops // 4,
    )(parts)
    upper_message = shifted(message, "replica", -1)
    column_products = call(products_kernel, (products, rounded_products), 400 * flops)
    upper_products, rounded_upper = column_products(upper_message, window)
    previous_products = shifted(rounded_upper, "replica", 1)
    message, _ = lax.optimization_barrier((message, rounded_upper))
    lower_products, rounded_lower = column_products(message, window)
    next_products = shifted(rounded_lower, "replica", -1)
    left = call(left_kernel, whole(bf16, mats, row_count, 6 * rank), flops // 4)(upper_message, lower_basis)
    pieces = 2 if row_count % 32 == 0 else 1
    updated, factors = call(
        update_kernel,
        (whole(bf16, mats, 1, row_count, columns), whole(f32, mats, 1, rank, columns)),
        4 * flops,
        out_specs=[pl.BlockSpec(memory_space=pl.ANY)] * 2,
        scratch_shapes=[
            pltpu.VMEM((mats, row_count, columns), bf16),
            pltpu.VMEM((mats, 1, rank, columns), f32),
            pltpu.SemaphoreType.DMA((mats, pieces + 1)),
        ],
    )(left, upper_products, next_products, lower_products, previous_products, window)
    return (updated, factors)


def solution(mesh):
    placed = (P(None, "replica", None, "tensor"), P(None, "replica", None, "tensor"))
    return jax.shard_map(
        shards,
        mesh=mesh,
        in_specs=placed,
        out_specs=(P(None, "replica", None, "tensor"), P(None, "replica", None, "tensor")),
        check_vma=False,
    )
```

```python
import functools

import jax
import jax.numpy as jnp
from jax import lax
from jax.experimental import pallas as pl
from jax.experimental.pallas import tpu as pltpu
from jax.sharding import PartitionSpec as P

LANES = 128
ROWS_BY_ROWS = (((1,), (1,)), ((), ()))
IN_VMEM = pl.BlockSpec(memory_space=pltpu.VMEM)


def shifted(value, axis, steps):
    count = lax.axis_size(axis)
    pairs = [(source, (source + steps) % count) for source in range(count)]
    return lax.ppermute(value, axis, pairs)


def parity_shifts(axis, steps):
    count = lax.axis_size(axis)

    def over(parity):
        pairs = [
            (source, (source + steps) % count)
            for source in range(count)
            if (source + min(steps, 0)) % 2 == parity
        ]
        return lambda value: lax.ppermute(value, axis, pairs)

    return over(1), over(0)


def padded(size):
    return -(-size // LANES) * LANES


def images_of(vectors_ref, window_ref, mat):
    return lax.dot_general(
        vectors_ref[mat], window_ref[mat], ROWS_BY_ROWS, preferred_element_type=jnp.float32
    )


def round_kernel(vectors_hbm, rounded_ref, held_ref, sem):
    copy = pltpu.make_async_copy(vectors_hbm, held_ref, sem)
    copy.start()
    copy.wait()
    rounded_ref[...] = held_ref[...].astype(jnp.bfloat16)


def images_kernel(vectors_ref, window_ref, images_ref):
    mats, rank, _ = vectors_ref.shape
    for mat in range(mats):
        images_ref[mat * rank : (mat + 1) * rank] = images_of(vectors_ref, window_ref, mat)


def orthonormal_rows(gram, images, rank):
    mats = gram.shape[0] // rank
    grams = [gram[mat * rank : (mat + 1) * rank] for mat in range(mats)]
    rows = [images[mat * rank : (mat + 1) * rank] for mat in range(mats)]
    place = lax.broadcasted_iota(jnp.int32, (rank, 1), 0)
    pivots = [jnp.ones((rank, 1), jnp.float32) for _ in range(mats)]
    for step in range(rank):
        for mat in range(mats):
            column = grams[mat][:, mat * rank + step : mat * rank + step + 1]
            pivot = column[step : step + 1]
            pivots[mat] = jnp.where(place == step, pivot, pivots[mat])
            if step < rank - 1:
                factor = jnp.where(place > step, column / pivot, 0.0)
                rows[mat] = rows[mat] - factor * rows[mat][step : step + 1]
                grams[mat] = grams[mat] - factor * grams[mat][step : step + 1]
    return jnp.concatenate([row / jnp.sqrt(pivot) for row, pivot in zip(rows, pivots)], 0)


def split(value):
    high = value.astype(jnp.bfloat16).astype(jnp.float32)
    return high, value - high


def basis_kernel(mats, parts_ref, basis_ref, message_ref):
    rank = parts_ref.shape[1] // mats
    row_count = parts_ref.shape[2]
    images = jnp.sum(parts_ref[...], 0)
    gram = lax.dot_general(
        images, images, ROWS_BY_ROWS, precision=lax.Precision.HIGHEST, preferred_element_type=jnp.float32
    )
    basis = orthonormal_rows(gram, images, rank)
    basis_ref[...] = basis
    high, low = split(basis)
    message_ref[:, :row_count] = high.astype(jnp.bfloat16)
    start = padded(row_count)
    message_ref[:, start : start + row_count] = low.astype(jnp.bfloat16)


def odd_replica():
    return lax.rem(lax.axis_index("replica"), 2) == 1


def products_into(basis_ref, window_ref, products_ref, rounded_ref):
    mats, row_count, _ = window_ref.shape
    rank = products_ref.shape[0] // mats
    basis = basis_ref[:, :row_count].astype(jnp.float32)
    for mat in range(mats):
        rows = slice(mat * rank, (mat + 1) * rank)
        products_ref[rows] = jnp.dot(
            basis[rows].astype(jnp.bfloat16), window_ref[mat], preferred_element_type=jnp.float32
        )
    rounded_ref[...] = products_ref[...].astype(jnp.bfloat16)


def lower_products_kernel(message_ref, window_ref, products_ref, rounded_ref):
    products_into(message_ref, window_ref, products_ref, rounded_ref)


def upper_products_kernel(odd, message_ref, window_ref, products_ref, rounded_ref):
    @pl.when(odd_replica() == odd)
    def _():
        products_into(message_ref, window_ref, products_ref, rounded_ref)


def left_kernel(odd_ref, even_ref, basis_ref, left_ref):
    mats, row_count, _ = left_ref.shape
    rank = basis_ref.shape[0] // mats
    start = padded(row_count)
    odd = odd_replica()
    upper_high, upper_low = (
        -0.5 * jnp.where(odd, odd_ref[:, own].astype(jnp.float32), even_ref[:, own].astype(jnp.float32))
        for own in (slice(0, row_count), slice(start, start + row_count))
    )
    lower_high, lower_low = split(0.5 * basis_ref[...])
    for mat in range(mats):
        rows = slice(mat * rank, (mat + 1) * rank)
        parts = [upper_high[rows], upper_low[rows], upper_high[rows], lower_high[rows], lower_low[rows], lower_high[rows]]
        left_ref[mat] = jnp.concatenate(parts, 0).T.astype(jnp.bfloat16)


def update_kernel(
    left_ref,
    odd_upper_ref,
    even_upper_ref,
    odd_next_ref,
    even_next_ref,
    lower_ref,
    odd_previous_ref,
    even_previous_ref,
    window_ref,
    updated_ref,
    factors_ref,
    held_ref,
    sums_ref,
    sems,
):
    mats, row_count, columns = window_ref.shape
    rank = lower_ref.shape[0] // mats
    width = 2 * LANES
    pieces = sems.shape[1] - 1
    piece = row_count // pieces
    odd = odd_replica()

    def chosen(if_odd, if_even, start, stop):
        picked = jnp.where(
            odd, if_odd[:, start:stop].astype(jnp.float32), if_even[:, start:stop].astype(jnp.float32)
        )
        return picked[rows]

    copies = []
    for mat in range(mats):
        rows = slice(mat * rank, (mat + 1) * rank)
        rights = []
        for start in range(0, columns, width):
            stop = min(start + width, columns)
            upper = chosen(odd_upper_ref, even_upper_ref, start, stop) - chosen(
                odd_next_ref, even_next_ref, start, stop
            )
            sums_ref[mat, 0, :, start:stop] = upper
            upper_high, upper_low = split(upper)
            lower = chosen(even_previous_ref, odd_previous_ref, start, stop) - lower_ref[rows, start:stop]
            lower_high, lower_low = split(lower)
            parts = [upper_high, upper_high, upper_low, lower_high, lower_high, lower_low]
            rights.append((start, stop, jnp.concatenate(parts, 0).astype(jnp.bfloat16)))
        copies.append(pltpu.make_async_copy(sums_ref.at[mat], factors_ref.at[mat], sems.at[mat, pieces]))
        copies[-1].start()
        for index in range(pieces):
            own = slice(index * piece, (index + 1) * piece)
            left = left_ref[mat, own]
            for start, stop, right in rights:
                change = jnp.dot(left, right, preferred_element_type=jnp.float32)
                held_ref[mat, own, start:stop] = (
                    window_ref[mat, own, start:stop].astype(jnp.float32) + change
                ).astype(jnp.bfloat16)
            copies.append(
                pltpu.make_async_copy(held_ref.at[mat, own], updated_ref.at[mat, 0, own], sems.at[mat, index])
            )
            copies[-1].start()
    for copy in copies:
        copy.wait()


def call(kernel, outs, flops, in_specs=None, out_specs=None, **more):
    def run(*operands):
        return pl.pallas_call(
            kernel,
            out_shape=outs,
            in_specs=[IN_VMEM] * len(operands) if in_specs is None else in_specs,
            out_specs=jax.tree.map(lambda _: IN_VMEM, outs) if out_specs is None else out_specs,
            cost_estimate=pl.CostEstimate(flops=flops, bytes_accessed=1 << 20, transcendentals=0),
            compiler_params=pltpu.CompilerParams(vmem_limit_bytes=24 << 20),
            **more,
        )(*operands)

    return run


def shards(weights, vectors):
    window = weights[:, 0]
    own_vectors = vectors[:, 0]
    mats, rank, columns = own_vectors.shape
    row_count = window.shape[1]
    stacked = mats * rank
    flops = 2 * stacked * row_count * columns

    def whole(dtype, *dims):
        return jax.ShapeDtypeStruct(dims, dtype)

    f32, bf16 = jnp.float32, jnp.bfloat16
    images = whole(f32, stacked, row_count)
    rounded_images = whole(bf16, stacked, row_count)
    products = whole(f32, stacked, columns)
    rounded_products = whole(bf16, stacked, columns)

    vectors_b = call(
        round_kernel,
        whole(bf16, *own_vectors.shape),
        100 * flops,
        in_specs=[pl.BlockSpec(memory_space=pltpu.HBM)],
        scratch_shapes=[pltpu.VMEM(own_vectors.shape, f32), pltpu.SemaphoreType.DMA],
    )(pltpu.with_memory_space_constraint(own_vectors, pltpu.HBM))
    left_vectors = shifted(vectors_b, "replica", 1)
    own_images = call(images_kernel, images, flops)(vectors_b, window)
    left_images = shifted(own_images, "replica", 1)
    next_images = call(images_kernel, images, flops)(left_vectors, window)
    group = lax.axis_size("tensor")
    parts = lax.all_to_all(
        jnp.broadcast_to((left_images - next_images)[None], (group, stacked, row_count)), "tensor", 0, 0
    )
    lower_basis, message = call(
        functools.partial(basis_kernel, mats),
        (images, whole(bf16, stacked, padded(row_count) + row_count)),
        flops // 4,
    )(parts)
    odd_down, even_down = parity_shifts("replica", -1)
    odd_up, even_up = parity_shifts("replica", 1)
    products_outs = (products, rounded_products)

    odd_basis = odd_down(message)
    lower_products, rounded = call(lower_products_kernel, products_outs, 400 * flops)(message, window)
    odd_next = odd_down(rounded)
    message, rounded = lax.optimization_barrier((message, rounded))
    even_basis = even_down(message)
    odd_upper, rounded_upper = call(functools.partial(upper_products_kernel, True), products_outs, 400 * flops)(
        odd_basis, window
    )
    odd_previous = odd_up(rounded_upper)
    even_upper, rounded_upper = call(functools.partial(upper_products_kernel, False), products_outs, 400 * flops)(
        even_basis, window
    )
    even_previous = even_up(rounded_upper)
    rounded, _ = lax.optimization_barrier((rounded, rounded_upper))
    even_next = even_down(rounded)
    left = call(left_kernel, whole(bf16, mats, row_count, 6 * rank), flops // 4)(odd_basis, even_basis, lower_basis)
    pieces = 2 if row_count % 32 == 0 else 1
    updated, factors = call(
        update_kernel,
        (whole(bf16, mats, 1, row_count, columns), whole(f32, mats, 1, rank, columns)),
        4 * flops,
        out_specs=[pl.BlockSpec(memory_space=pl.ANY)] * 2,
        scratch_shapes=[
            pltpu.VMEM((mats, row_count, columns), bf16),
            pltpu.VMEM((mats, 1, rank, columns), f32),
            pltpu.SemaphoreType.DMA((mats, pieces + 1)),
        ],
    )(
        left,
        odd_upper,
        even_upper,
        odd_next,
        even_next,
        lower_products,
        odd_previous,
        even_previous,
        window,
    )
    return (updated, factors)


def solution(mesh):
    placed = (P(None, "replica", None, "tensor"), P(None, "replica", None, "tensor"))
    return jax.shard_map(
        shards,
        mesh=mesh,
        in_specs=placed,
        out_specs=(P(None, "replica", None, "tensor"), P(None, "replica", None, "tensor")),
        check_vma=False,
    )
```

```python
import functools

import jax
import jax.numpy as jnp
from jax import lax
from jax.experimental import pallas as pl
from jax.experimental.pallas import tpu as pltpu
from jax.sharding import PartitionSpec as P

LANES = 128
ROWS_BY_ROWS = (((1,), (1,)), ((), ()))
IN_VMEM = pl.BlockSpec(memory_space=pltpu.VMEM)


def shifted(value, axis, steps):
    count = lax.axis_size(axis)
    return lax.ppermute(value, axis, [(source, (source + steps) % count) for source in range(count)])


def parity_shifts(axis, steps):
    count = lax.axis_size(axis)

    def over(parity):
        pairs = [
            (source, (source + steps) % count)
            for source in range(count)
            if (source + min(steps, 0)) % 2 == parity
        ]
        return lambda value: lax.ppermute(value, axis, pairs)

    return over(1), over(0)


def padded(size):
    return -(-size // LANES) * LANES


def odd_replica():
    return lax.rem(lax.axis_index("replica"), 2) == 1


def images_kernel(vectors_ref, window_ref, images_ref):
    mats, rank, _ = vectors_ref.shape
    for mat in range(mats):
        images_ref[mat * rank : (mat + 1) * rank] = lax.dot_general(
            vectors_ref[mat], window_ref[mat], ROWS_BY_ROWS, preferred_element_type=jnp.float32
        )


def round_kernel(vectors_hbm, rounded_ref, held_ref, sem):
    copy = pltpu.make_async_copy(vectors_hbm, held_ref, sem)
    copy.start()
    copy.wait()
    rounded_ref[...] = held_ref[...].astype(jnp.bfloat16)


def own_images_kernel(vectors_ref, window_ref, images_ref, vectors_out_ref):
    mats, rank, _ = vectors_ref.shape
    vectors_out_ref[...] = vectors_ref[...]
    for mat in range(mats):
        images_ref[mat * rank : (mat + 1) * rank] = images_of(vectors_ref[mat], window_ref[mat])


def differences_kernel(
    even_images_ref, even_vectors_ref, odd_images_ref, odd_vectors_ref, window_ref, differences_ref
):
    mats, rank, _ = odd_vectors_ref.shape
    odd = odd_replica()

    def chosen(if_odd, if_even):
        return jnp.where(odd, if_odd.astype(jnp.float32), if_even.astype(jnp.float32))

    for mat in range(mats):
        rows = slice(mat * rank, (mat + 1) * rank)
        vectors = chosen(even_vectors_ref[mat], odd_vectors_ref[mat]).astype(jnp.bfloat16)
        images = chosen(even_images_ref[rows], odd_images_ref[rows])
        differences_ref[rows] = images - images_of(vectors, window_ref[mat])


def round_kernel(vectors_hbm, rounded_ref, held_ref, sem):
    copy = pltpu.make_async_copy(vectors_hbm, held_ref, sem)
    copy.start()
    copy.wait()
    rounded_ref[...] = held_ref[...].astype(jnp.bfloat16)


def own_images_kernel(vectors_ref, window_ref, images_ref, vectors_out_ref):
    mats, rank, _ = vectors_ref.shape
    vectors_out_ref[...] = vectors_ref[...]
    for mat in range(mats):
        images_ref[mat * rank : (mat + 1) * rank] = images_of(vectors_ref[mat], window_ref[mat])


def next_images_kernel(even_ref, odd_ref, window_ref, images_ref):
    mats, rank, _ = odd_ref.shape
    odd = odd_replica()
    for mat in range(mats):
        vectors = jnp.where(odd, even_ref[mat].astype(jnp.float32), odd_ref[mat].astype(jnp.float32))
        images_ref[mat * rank : (mat + 1) * rank] = images_of(vectors.astype(jnp.bfloat16), window_ref[mat])


def orthonormal_rows(gram, images, rank):
    mats = gram.shape[0] // rank
    grams = [gram[mat * rank : (mat + 1) * rank] for mat in range(mats)]
    rows = [images[mat * rank : (mat + 1) * rank] for mat in range(mats)]
    place = lax.broadcasted_iota(jnp.int32, (rank, 1), 0)
    pivots = [jnp.ones((rank, 1), jnp.float32) for _ in range(mats)]
    for step in range(rank):
        for mat in range(mats):
            column = grams[mat][:, mat * rank + step : mat * rank + step + 1]
            pivot = column[step : step + 1]
            pivots[mat] = jnp.where(place == step, pivot, pivots[mat])
            if step < rank - 1:
                factor = jnp.where(place > step, column / pivot, 0.0)
                rows[mat] = rows[mat] - factor * rows[mat][step : step + 1]
                grams[mat] = grams[mat] - factor * grams[mat][step : step + 1]
    return jnp.concatenate([row / jnp.sqrt(pivot) for row, pivot in zip(rows, pivots)], 0)


def split(value):
    high = value.astype(jnp.bfloat16).astype(jnp.float32)
    return high, value - high


def basis_kernel(mats, parts_ref, basis_ref, message_ref):
    rank = parts_ref.shape[1] // mats
    row_count = parts_ref.shape[2]
    images = jnp.sum(parts_ref[...], 0)
    gram = lax.dot_general(
        images, images, ROWS_BY_ROWS, precision=lax.Precision.HIGHEST, preferred_element_type=jnp.float32
    )
    basis = orthonormal_rows(gram, images, rank)
    basis_ref[...] = basis
    high, low = split(basis)
    message_ref[:, :row_count] = high.astype(jnp.bfloat16)
    start = padded(row_count)
    message_ref[:, start : start + row_count] = low.astype(jnp.bfloat16)


def products_into(basis_ref, window_ref, products_ref, rounded_ref):
    mats, row_count, _ = window_ref.shape
    rank = products_ref.shape[0] // mats
    basis = basis_ref[:, :row_count].astype(jnp.float32)
    for mat in range(mats):
        rows = slice(mat * rank, (mat + 1) * rank)
        products_ref[rows] = jnp.dot(
            basis[rows].astype(jnp.bfloat16), window_ref[mat], preferred_element_type=jnp.float32
        )
    rounded_ref[...] = products_ref[...].astype(jnp.bfloat16)


def lower_products_kernel(basis_ref, window_ref, products_ref, message_ref):
    columns = products_ref.shape[1]
    products_into(basis_ref, window_ref, products_ref, message_ref.at[:, :columns])
    message_ref[:, padded(columns) :] = basis_ref[...]


def upper_products_kernel(odd, start, message_ref, window_ref, products_ref, rounded_ref):
    @pl.when(odd_replica() == odd)
    def _():
        products_into(message_ref.at[:, start:], window_ref, products_ref, rounded_ref)


def factors_kernel(
    message_ref,
    odd_products_ref,
    even_products_ref,
    lower_basis_ref,
    lower_products_ref,
    left_ref,
    right_ref,
    factors_hbm,
    factors_ref,
    sem,
):
    mats, row_count, _ = left_ref.shape
    stacked, columns = lower_products_ref.shape
    rank = stacked // mats
    upper = jnp.where(odd_replica(), odd_products_ref[...], even_products_ref[...]) - message_ref[
        :, :columns
    ].astype(jnp.float32)
    for mat in range(mats):
        factors_ref[mat, 0] = upper[mat * rank : (mat + 1) * rank]
    copy = pltpu.make_async_copy(factors_ref, factors_hbm, sem)
    copy.start()
    high, low = padded(columns), padded(columns) + padded(row_count)
    upper_high = -0.5 * message_ref[:, high : high + row_count].astype(jnp.float32)
    upper_low = -0.5 * message_ref[:, low : low + row_count].astype(jnp.float32)
    lower_high, lower_low = split(0.5 * lower_basis_ref[...])
    factor_high, factor_low = split(upper)
    products_high, products_low = split(-lower_products_ref[...])
    for mat in range(mats):
        rows = slice(mat * rank, (mat + 1) * rank)
        lefts = [upper_high, upper_low, upper_high, lower_high, lower_low, lower_high, lower_high, lower_low]
        left_ref[mat] = jnp.concatenate([part[rows] for part in lefts], 0).T.astype(jnp.bfloat16)
        rights = [factor_high, factor_high, factor_low, products_high, products_high, products_low]
        right_ref[mat] = jnp.concatenate([part[rows] for part in rights], 0).astype(jnp.bfloat16)
    copy.wait()


def update_kernel(left_ref, right_ref, odd_ref, even_ref, window_ref, updated_ref, held_ref, sems):
    mats, _, columns = window_ref.shape
    rank = odd_ref.shape[0] // mats
    width = 2 * LANES
    odd = odd_replica()
    copies = []
    for mat in range(mats):
        rows = slice(mat * rank, (mat + 1) * rank)
        for start in range(0, columns, width):
            stop = min(start + width, columns)
            lower = jnp.where(
                odd, even_ref[:, start:stop].astype(jnp.float32), odd_ref[:, start:stop].astype(jnp.float32)
            )[rows]
            last = jnp.concatenate([lower, lower], 0).astype(jnp.bfloat16)
            right = jnp.concatenate([right_ref[mat, :, start:stop], last], 0)
            change = jnp.dot(left_ref[mat], right, preferred_element_type=jnp.float32)
            held_ref[mat, :, start:stop] = (window_ref[mat, :, start:stop].astype(jnp.float32) + change).astype(
                jnp.bfloat16
            )
        copies.append(pltpu.make_async_copy(held_ref.at[mat], updated_ref.at[mat, 0], sems.at[mat]))
        copies[-1].start()
    for copy in copies:
        copy.wait()


def call(kernel, outs, flops, in_specs=None, out_specs=None, **more):
    def run(*operands):
        return pl.pallas_call(
            kernel,
            out_shape=outs,
            in_specs=[IN_VMEM] * len(operands) if in_specs is None else in_specs,
            out_specs=jax.tree.map(lambda _: IN_VMEM, outs) if out_specs is None else out_specs,
            cost_estimate=pl.CostEstimate(flops=flops, bytes_accessed=1 << 20, transcendentals=0),
            compiler_params=pltpu.CompilerParams(vmem_limit_bytes=24 << 20),
            **more,
        )(*operands)

    return run


def shards(weights, vectors):
    window = weights[:, 0]
    own_vectors = vectors[:, 0]
    mats, rank, columns = own_vectors.shape
    row_count = window.shape[1]
    stacked = mats * rank
    flops = 2 * stacked * row_count * columns

    def whole(dtype, *dims):
        return jax.ShapeDtypeStruct(dims, dtype)

    f32, bf16 = jnp.float32, jnp.bfloat16
    images = whole(f32, stacked, row_count)
    rounded_images = whole(bf16, stacked, row_count)
    products = whole(f32, stacked, columns)
    rounded_products = whole(bf16, stacked, columns)

    vectors_b = call(
        round_kernel,
        whole(bf16, *own_vectors.shape),
        100 * flops,
        in_specs=[pl.BlockSpec(memory_space=pltpu.HBM)],
        scratch_shapes=[pltpu.VMEM(own_vectors.shape, f32), pltpu.SemaphoreType.DMA],
    )(pltpu.with_memory_space_constraint(own_vectors, pltpu.HBM))
    left_vectors = shifted(vectors_b, "replica", 1)
    own_images = call(images_kernel, images, flops)(vectors_b, window)
    left_images = shifted(own_images, "replica", 1)
    next_images = call(images_kernel, images, flops)(left_vectors, window)
    group = lax.axis_size("tensor")
    parts = lax.all_to_all(
        jnp.broadcast_to((left_images - next_images)[None], (group, stacked, row_count)), "tensor", 0, 0
    )
    lower_basis, basis = call(
        functools.partial(basis_kernel, mats),
        (images, whole(bf16, stacked, padded(row_count) + row_count)),
        flops // 4,
    )(parts)
    products_outs = (products, rounded_products)
    base = padded(columns)
    odd_up, even_up = parity_shifts("replica", 1)
    odd_down, _ = parity_shifts("replica", -1)

    odd_basis = odd_down(basis)
    lower_products, message = call(
        lower_products_kernel, (products, whole(bf16, stacked, base + basis.shape[1])), 400 * flops
    )(basis, window)
    message = shifted(message, "replica", -1)
    odd_upper, rounded_upper = call(functools.partial(upper_products_kernel, True, 0), products_outs, 400 * flops)(
        odd_basis, window
    )
    odd_previous = odd_up(rounded_upper)
    even_upper, rounded_upper = call(functools.partial(upper_products_kernel, False, base), products_outs, 0)(
        message, window
    )
    even_previous = even_up(rounded_upper)
    left, right, factors = call(
        factors_kernel,
        (
            whole(bf16, mats, row_count, 8 * rank),
            whole(bf16, mats, 6 * rank, columns),
            whole(f32, mats, 1, rank, columns),
        ),
        flops // 4,
        out_specs=(IN_VMEM, IN_VMEM, pl.BlockSpec(memory_space=pl.ANY)),
        scratch_shapes=[pltpu.VMEM((mats, 1, rank, columns), f32), pltpu.SemaphoreType.DMA],
    )(message, odd_upper, even_upper, lower_basis, lower_products)
    updated = call(
        update_kernel,
        whole(bf16, mats, 1, row_count, columns),
        4 * flops,
        out_specs=pl.BlockSpec(memory_space=pl.ANY),
        scratch_shapes=[pltpu.VMEM((mats, row_count, columns), bf16), pltpu.SemaphoreType.DMA((mats,))],
    )(left, right, odd_previous, even_previous, window)
    return (updated, factors)


def solution(mesh):
    placed = (P(None, "replica", None, "tensor"), P(None, "replica", None, "tensor"))
    return jax.shard_map(
        shards,
        mesh=mesh,
        in_specs=placed,
        out_specs=(P(None, "replica", None, "tensor"), P(None, "replica", None, "tensor")),
        check_vma=False,
    )
```

```python
import functools

import jax
import jax.numpy as jnp
from jax import lax
from jax.experimental import pallas as pl
from jax.experimental.pallas import tpu as pltpu
from jax.sharding import PartitionSpec as P

LANES = 128
ROWS_BY_ROWS = (((1,), (1,)), ((), ()))
IN_VMEM = pl.BlockSpec(memory_space=pltpu.VMEM)


def shifted(value, axis, steps):
    count = lax.axis_size(axis)
    return lax.ppermute(value, axis, [(source, (source + steps) % count) for source in range(count)])


def parity_shifts(axis, steps):
    count = lax.axis_size(axis)

    def over(parity):
        pairs = [
            (source, (source + steps) % count)
            for source in range(count)
            if (source + min(steps, 0)) % 2 == parity
        ]
        return lambda value: lax.ppermute(value, axis, pairs)

    return over(1), over(0)


def padded(size):
    return -(-size // LANES) * LANES


def odd_replica():
    return lax.rem(lax.axis_index("replica"), 2) == 1


def images_of(vectors, window_ref, mat):
    return lax.dot_general(
        vectors.astype(jnp.bfloat16), window_ref[mat], ROWS_BY_ROWS, preferred_element_type=jnp.float32
    )


def own_images_kernel(vectors_ref, window_ref, images_ref, message_ref):
    mats, _, columns = vectors_ref.shape
    row_count = window_ref.shape[1]
    images = jnp.concatenate([images_of(vectors_ref[mat], window_ref, mat) for mat in range(mats)], 0)
    images_ref[...] = images
    vectors = jnp.concatenate([vectors_ref[mat].astype(jnp.float32) for mat in range(mats)], 0)
    message_ref[:, :columns] = vectors.astype(jnp.bfloat16)
    for part in range(3):
        start = padded(columns) + part * padded(row_count)
        high, images = split(images)
        message_ref[:, start : start + row_count] = high.astype(jnp.bfloat16)


def odd_images_kernel(vectors_ref, window_ref, images_ref):
    mats, rank, _ = vectors_ref.shape

    @pl.when(jnp.logical_not(odd_replica()))
    def _():
        for mat in range(mats):
            images_ref[mat * rank : (mat + 1) * rank] = images_of(vectors_ref[mat], window_ref, mat)


def differences_kernel(even_message_ref, odd_left_ref, odd_images_ref, window_ref, differences_ref):
    mats, row_count, columns = window_ref.shape
    rank = odd_images_ref.shape[0] // mats

    @pl.when(odd_replica())
    def _():
        starts = [padded(columns) + part * padded(row_count) for part in range(3)]
        high, middle, low = (
            even_message_ref[:, start : start + row_count].astype(jnp.float32) for start in starts
        )
        left_images = high + (middle + low)
        vectors = even_message_ref[:, :columns].astype(jnp.float32)
        for mat in range(mats):
            rows = slice(mat * rank, (mat + 1) * rank)
            differences_ref[rows] = left_images[rows] - images_of(vectors[rows], window_ref, mat)

    @pl.when(jnp.logical_not(odd_replica()))
    def _():
        differences_ref[...] = odd_left_ref[...] - odd_images_ref[...]


def round_kernel(vectors_hbm, rounded_ref, held_ref, sem):
    copy = pltpu.make_async_copy(vectors_hbm, held_ref, sem)
    copy.start()
    copy.wait()
    rounded_ref[...] = held_ref[...].astype(jnp.bfloat16)


def orthonormal_rows(gram, images, rank):
    mats = gram.shape[0] // rank
    count = images.shape[1]

    def column(mat, step):
        at = mat * rank + step
        return jnp.broadcast_to(gram[mat * rank : (mat + 1) * rank, at : at + 1], (rank, LANES))

    def widened(value):
        return jnp.concatenate([value] * (padded(count) // LANES), 1)[:, :count]

    place = lax.broadcasted_iota(jnp.int32, (rank, LANES), 0)
    columns = [[column(mat, step) for step in range(rank)] for mat in range(mats)]
    rows = [images[mat * rank : (mat + 1) * rank] for mat in range(mats)]
    pivots = [jnp.ones((rank, LANES), jnp.float32) for _ in range(mats)]
    for step in range(rank):
        for mat in range(mats):
            pivot = columns[mat][step][step : step + 1]
            pivots[mat] = jnp.where(place == step, pivot, pivots[mat])
            factor = jnp.where(place > step, columns[mat][step] / pivot, 0.0)
            for later in range(step + 1, rank):
                columns[mat][later] = columns[mat][later] - factor * columns[mat][later][step : step + 1]
            if step < rank - 1:
                rows[mat] = rows[mat] - widened(factor) * rows[mat][step : step + 1]
    return jnp.concatenate([row / widened(jnp.sqrt(pivot)) for row, pivot in zip(rows, pivots)], 0)


def split(value):
    high = value.astype(jnp.bfloat16).astype(jnp.float32)
    return high, value - high


def products_into(basis_ref, window_ref, products_ref, rounded_ref):
    mats, row_count, _ = window_ref.shape
    rank = products_ref.shape[0] // mats
    basis = basis_ref[:, :row_count].astype(jnp.float32)
    for mat in range(mats):
        rows = slice(mat * rank, (mat + 1) * rank)
        products_ref[rows] = jnp.dot(
            basis[rows].astype(jnp.bfloat16), window_ref[mat], preferred_element_type=jnp.float32
        )
    rounded_ref[...] = products_ref[...].astype(jnp.bfloat16)


def lower_products(basis_ref, window_ref, products_ref, message_ref):
    columns = products_ref.shape[1]
    products_into(basis_ref, window_ref, products_ref, message_ref.at[:, :columns])
    message_ref[:, padded(columns) :] = basis_ref[...]


def basis_kernel(parts_ref, window_ref, basis_ref, parts_out_ref, products_ref, message_ref):
    rank = parts_ref.shape[1] // window_ref.shape[0]
    row_count = parts_ref.shape[2]
    images = jnp.sum(parts_ref[...], 0)
    gram = lax.dot_general(
        images, images, ROWS_BY_ROWS, precision=lax.Precision.HIGHEST, preferred_element_type=jnp.float32
    )
    basis = orthonormal_rows(gram, images, rank)
    basis_ref[...] = basis
    high, low = split(basis)
    parts_out_ref[:, :row_count] = high.astype(jnp.bfloat16)
    start = padded(row_count)
    parts_out_ref[:, start : start + row_count] = low.astype(jnp.bfloat16)

    @pl.when(jnp.logical_not(odd_replica()))
    def _():
        lower_products(parts_out_ref, window_ref, products_ref, message_ref)


def odd_products_kernel(basis_ref, window_ref, _, __, products_ref, message_ref):
    @pl.when(odd_replica())
    def _():
        lower_products(basis_ref, window_ref, products_ref, message_ref)


def upper_products_kernel(odd, start, message_ref, window_ref, products_ref, rounded_ref):
    @pl.when(odd_replica() == odd)
    def _():
        products_into(message_ref.at[:, start:], window_ref, products_ref, rounded_ref)


def factors_kernel(
    message_ref,
    odd_products_ref,
    even_products_ref,
    lower_basis_ref,
    lower_products_ref,
    left_ref,
    right_ref,
    factors_hbm,
    factors_ref,
    sem,
):
    mats, row_count, _ = left_ref.shape
    stacked, columns = lower_products_ref.shape
    rank = stacked // mats
    upper = jnp.where(odd_replica(), odd_products_ref[...], even_products_ref[...]) - message_ref[
        :, :columns
    ].astype(jnp.float32)
    for mat in range(mats):
        factors_ref[mat, 0] = upper[mat * rank : (mat + 1) * rank]
    copy = pltpu.make_async_copy(factors_ref, factors_hbm, sem)
    copy.start()
    high, low = padded(columns), padded(columns) + padded(row_count)
    upper_high = -0.5 * message_ref[:, high : high + row_count].astype(jnp.float32)
    upper_low = -0.5 * message_ref[:, low : low + row_count].astype(jnp.float32)
    lower_high, lower_low = split(0.5 * lower_basis_ref[...])
    factor_high, factor_low = split(upper)
    products_high, products_low = split(-lower_products_ref[...])
    for mat in range(mats):
        rows = slice(mat * rank, (mat + 1) * rank)
        lefts = [upper_high, upper_low, upper_high, lower_high, lower_low, lower_high, lower_high, lower_low]
        left_ref[mat] = jnp.concatenate([part[rows] for part in lefts], 0).T.astype(jnp.bfloat16)
        rights = [factor_high, factor_high, factor_low, products_high, products_high, products_low]
        right_ref[mat] = jnp.concatenate([part[rows] for part in rights], 0).astype(jnp.bfloat16)
    copy.wait()


def update_kernel(left_ref, right_ref, odd_ref, even_ref, window_ref, updated_ref, held_ref, sems):
    mats, _, columns = window_ref.shape
    rank = odd_ref.shape[0] // mats
    width = 2 * LANES
    odd = odd_replica()
    copies = []
    for mat in range(mats):
        rows = slice(mat * rank, (mat + 1) * rank)
        for start in range(0, columns, width):
            stop = min(start + width, columns)
            lower = jnp.where(
                odd, even_ref[:, start:stop].astype(jnp.float32), odd_ref[:, start:stop].astype(jnp.float32)
            )[rows]
            last = jnp.concatenate([lower, lower], 0).astype(jnp.bfloat16)
            right = jnp.concatenate([right_ref[mat, :, start:stop], last], 0)
            change = jnp.dot(left_ref[mat], right, preferred_element_type=jnp.float32)
            held_ref[mat, :, start:stop] = (window_ref[mat, :, start:stop].astype(jnp.float32) + change).astype(
                jnp.bfloat16
            )
        copies.append(pltpu.make_async_copy(held_ref.at[mat], updated_ref.at[mat, 0], sems.at[mat]))
        copies[-1].start()
    for copy in copies:
        copy.wait()


def call(kernel, outs, flops, in_specs=None, out_specs=None, **more):
    def run(*operands):
        return pl.pallas_call(
            kernel,
            out_shape=outs,
            in_specs=[IN_VMEM] * len(operands) if in_specs is None else in_specs,
            out_specs=jax.tree.map(lambda _: IN_VMEM, outs) if out_specs is None else out_specs,
            cost_estimate=pl.CostEstimate(flops=flops, bytes_accessed=1 << 20, transcendentals=0),
            compiler_params=pltpu.CompilerParams(vmem_limit_bytes=24 << 20),
            **more,
        )(*operands)

    return run


def shards(weights, vectors):
    window = weights[:, 0]
    own_vectors = vectors[:, 0]
    mats, rank, columns = own_vectors.shape
    row_count = window.shape[1]
    stacked = mats * rank
    flops = 2 * stacked * row_count * columns

    def whole(dtype, *dims):
        return jax.ShapeDtypeStruct(dims, dtype)

    f32, bf16 = jnp.float32, jnp.bfloat16
    images = whole(f32, stacked, row_count)
    rounded_images = whole(bf16, stacked, row_count)
    products = whole(f32, stacked, columns)
    rounded_products = whole(bf16, stacked, columns)

    vectors_b = call(
        round_kernel,
        whole(bf16, *own_vectors.shape),
        100 * flops,
        in_specs=[pl.BlockSpec(memory_space=pltpu.HBM)],
        scratch_shapes=[pltpu.VMEM(own_vectors.shape, f32), pltpu.SemaphoreType.DMA],
    )(pltpu.with_memory_space_constraint(own_vectors, pltpu.HBM))
    odd_up, even_up = parity_shifts("replica", 1)
    odd_down, _ = parity_shifts("replica", -1)
    base = padded(columns)
    odd_vectors = odd_up(vectors_b)
    own_images, message = call(
        own_images_kernel, (images, whole(bf16, stacked, base + 2 * padded(row_count) + row_count)), 400 * flops
    )(vectors_b, window)
    odd_left = odd_up(own_images)
    even_message = even_up(message)
    odd_images = call(odd_images_kernel, images, 400 * flops)(odd_vectors, window)
    differences = call(differences_kernel, images, flops)(even_message, odd_left, odd_images, window)
    group = lax.axis_size("tensor")
    parts = lax.all_to_all(
        jnp.broadcast_to(differences[None], (group, stacked, row_count)), "tensor", 0, 0
    )
    message_out = whole(bf16, stacked, base + padded(row_count) + row_count)
    lower_basis, basis, lower_products, message = call(
        basis_kernel,
        (images, whole(bf16, stacked, padded(row_count) + row_count), products, message_out),
        flops,
    )(parts, window)
    products_outs = (products, rounded_products)

    odd_basis = odd_down(basis)
    lower_products, message = call(
        odd_products_kernel, (products, message_out), 400 * flops, input_output_aliases={2: 0, 3: 1}
    )(basis, window, lower_products, message)
    message = shifted(message, "replica", -1)
    odd_upper, rounded_upper = call(functools.partial(upper_products_kernel, True, 0), products_outs, 400 * flops)(
        odd_basis, window
    )
    odd_previous = odd_up(rounded_upper)
    even_upper, rounded_upper = call(functools.partial(upper_products_kernel, False, base), products_outs, 0)(
        message, window
    )
    even_previous = even_up(rounded_upper)
    left, right, factors = call(
        factors_kernel,
        (
            whole(bf16, mats, row_count, 8 * rank),
            whole(bf16, mats, 6 * rank, columns),
            whole(f32, mats, 1, rank, columns),
        ),
        flops // 4,
        out_specs=(IN_VMEM, IN_VMEM, pl.BlockSpec(memory_space=pl.ANY)),
        scratch_shapes=[pltpu.VMEM((mats, 1, rank, columns), f32), pltpu.SemaphoreType.DMA],
    )(message, odd_upper, even_upper, lower_basis, lower_products)
    updated = call(
        update_kernel,
        whole(bf16, mats, 1, row_count, columns),
        4 * flops,
        out_specs=pl.BlockSpec(memory_space=pl.ANY),
        scratch_shapes=[pltpu.VMEM((mats, row_count, columns), bf16), pltpu.SemaphoreType.DMA((mats,))],
    )(left, right, odd_previous, even_previous, window)
    return (updated, factors)


def solution(mesh):
    placed = (P(None, "replica", None, "tensor"), P(None, "replica", None, "tensor"))
    return jax.shard_map(
        shards,
        mesh=mesh,
        in_specs=placed,
        out_specs=(P(None, "replica", None, "tensor"), P(None, "replica", None, "tensor")),
        check_vma=False,
    )
```

```python
import functools

import jax
import jax.numpy as jnp
from jax import lax
from jax.experimental import pallas as pl
from jax.experimental.pallas import tpu as pltpu
from jax.sharding import PartitionSpec as P

LANES = 128
ROWS_BY_ROWS = (((1,), (1,)), ((), ()))
IN_VMEM = pl.BlockSpec(memory_space=pltpu.VMEM)


def shifted(value, axis, steps):
    count = lax.axis_size(axis)
    return lax.ppermute(value, axis, [(source, (source + steps) % count) for source in range(count)])


def parity_shifts(axis, steps):
    count = lax.axis_size(axis)

    def over(parity):
        pairs = [
            (source, (source + steps) % count)
            for source in range(count)
            if (source + min(steps, 0)) % 2 == parity
        ]
        return lambda value: lax.ppermute(value, axis, pairs)

    return over(1), over(0)


def padded(size):
    return -(-size // LANES) * LANES


def odd_replica():
    return lax.rem(lax.axis_index("replica"), 2) == 1


def images_of(vectors, window_ref, mat):
    return lax.dot_general(
        vectors.astype(jnp.bfloat16), window_ref[mat], ROWS_BY_ROWS, preferred_element_type=jnp.float32
    )


def own_images_kernel(vectors_ref, window_ref, images_ref, message_ref):
    mats, row_count, columns = window_ref.shape
    rank = images_ref.shape[0] // mats
    vectors = vectors_ref[...].astype(jnp.float32)
    images = jnp.concatenate(
        [images_of(vectors[mat * rank : (mat + 1) * rank], window_ref, mat) for mat in range(mats)], 0
    )
    images_ref[...] = images

    @pl.when(jnp.logical_not(odd_replica()))
    def _():
        message_ref[:, :columns] = vectors_ref[...]
        rest = images
        for part in range(3):
            start = padded(columns) + part * padded(row_count)
            high, rest = split(rest)
            message_ref[:, start : start + row_count] = high.astype(jnp.bfloat16)


def odd_images_kernel(vectors_ref, window_ref, images_ref):
    mats = window_ref.shape[0]
    rank = images_ref.shape[0] // mats

    @pl.when(jnp.logical_not(odd_replica()))
    def _():
        vectors = vectors_ref[...].astype(jnp.float32)
        for mat in range(mats):
            rows = slice(mat * rank, (mat + 1) * rank)
            images_ref[rows] = images_of(vectors[rows], window_ref, mat)


def differences_kernel(even_message_ref, odd_left_ref, odd_images_ref, window_ref, differences_ref):
    mats, row_count, columns = window_ref.shape
    rank = odd_images_ref.shape[0] // mats

    @pl.when(odd_replica())
    def _():
        starts = [padded(columns) + part * padded(row_count) for part in range(3)]
        high, middle, low = (
            even_message_ref[:, start : start + row_count].astype(jnp.float32) for start in starts
        )
        left_images = high + (middle + low)
        vectors = even_message_ref[:, :columns].astype(jnp.float32)
        for mat in range(mats):
            rows = slice(mat * rank, (mat + 1) * rank)
            differences_ref[rows] = left_images[rows] - images_of(vectors[rows], window_ref, mat)

    @pl.when(jnp.logical_not(odd_replica()))
    def _():
        differences_ref[...] = odd_left_ref[...] - odd_images_ref[...]


def round_kernel(vectors_hbm, rounded_ref, held_ref, sem):
    copy = pltpu.make_async_copy(vectors_hbm, held_ref, sem)
    copy.start()
    copy.wait()
    mats = held_ref.shape[0]
    rounded_ref[...] = jnp.concatenate([held_ref[mat] for mat in range(mats)], 0).astype(jnp.bfloat16)


def orthonormal_rows(gram, images, rank):
    mats = gram.shape[0] // rank
    count = images.shape[1]

    def column(mat, step):
        at = mat * rank + step
        return jnp.broadcast_to(gram[mat * rank : (mat + 1) * rank, at : at + 1], (rank, LANES))

    def widened(value):
        return jnp.concatenate([value] * (padded(count) // LANES), 1)[:, :count]

    place = lax.broadcasted_iota(jnp.int32, (rank, LANES), 0)
    columns = [[column(mat, step) for step in range(rank)] for mat in range(mats)]
    rows = [images[mat * rank : (mat + 1) * rank] for mat in range(mats)]
    pivots = [jnp.ones((rank, LANES), jnp.float32) for _ in range(mats)]
    for step in range(rank):
        for mat in range(mats):
            pivot = columns[mat][step][step : step + 1]
            pivots[mat] = jnp.where(place == step, pivot, pivots[mat])
            factor = jnp.where(place > step, columns[mat][step] / pivot, 0.0)
            for later in range(step + 1, rank):
                columns[mat][later] = columns[mat][later] - factor * columns[mat][later][step : step + 1]
            if step < rank - 1:
                rows[mat] = rows[mat] - widened(factor) * rows[mat][step : step + 1]
    return jnp.concatenate([row / widened(jnp.sqrt(pivot)) for row, pivot in zip(rows, pivots)], 0)


def split(value):
    high = value.astype(jnp.bfloat16).astype(jnp.float32)
    return high, value - high


def products_into(basis_ref, window_ref, products_ref, rounded_ref):
    mats, row_count, _ = window_ref.shape
    rank = products_ref.shape[0] // mats
    basis = basis_ref[:, :row_count].astype(jnp.float32)
    for mat in range(mats):
        rows = slice(mat * rank, (mat + 1) * rank)
        products_ref[rows] = jnp.dot(
            basis[rows].astype(jnp.bfloat16), window_ref[mat], preferred_element_type=jnp.float32
        )
    rounded_ref[...] = products_ref[...].astype(jnp.bfloat16)


def lower_products(basis_ref, window_ref, products_ref, message_ref):
    columns = products_ref.shape[1]
    products_into(basis_ref, window_ref, products_ref, message_ref.at[:, :columns])
    message_ref[:, padded(columns) :] = basis_ref[...]


def basis_kernel(parts_ref, window_ref, basis_ref, parts_out_ref, products_ref, message_ref):
    rank = parts_ref.shape[1] // window_ref.shape[0]
    row_count = parts_ref.shape[2]
    images = jnp.sum(parts_ref[...], 0)
    gram = lax.dot_general(
        images, images, ROWS_BY_ROWS, precision=lax.Precision.HIGHEST, preferred_element_type=jnp.float32
    )
    basis = orthonormal_rows(gram, images, rank)
    basis_ref[...] = basis
    high, low = split(basis)
    parts_out_ref[:, :row_count] = high.astype(jnp.bfloat16)
    start = padded(row_count)
    parts_out_ref[:, start : start + row_count] = low.astype(jnp.bfloat16)

    @pl.when(jnp.logical_not(odd_replica()))
    def _():
        lower_products(parts_out_ref, window_ref, products_ref, message_ref)


def odd_products_kernel(basis_ref, window_ref, _, __, products_ref, message_ref):
    @pl.when(odd_replica())
    def _():
        lower_products(basis_ref, window_ref, products_ref, message_ref)


def upper_products_kernel(odd, start, message_ref, window_ref, products_ref, rounded_ref):
    @pl.when(odd_replica() == odd)
    def _():
        products_into(message_ref.at[:, start:], window_ref, products_ref, rounded_ref)


def factors_kernel(
    message_ref,
    odd_products_ref,
    even_products_ref,
    lower_basis_ref,
    lower_products_ref,
    left_ref,
    right_ref,
    factors_hbm,
    factors_ref,
    sem,
):
    mats, row_count, _ = left_ref.shape
    stacked, columns = lower_products_ref.shape
    rank = stacked // mats
    upper = jnp.where(odd_replica(), odd_products_ref[...], even_products_ref[...]) - message_ref[
        :, :columns
    ].astype(jnp.float32)
    for mat in range(mats):
        factors_ref[mat, 0] = upper[mat * rank : (mat + 1) * rank]
    copy = pltpu.make_async_copy(factors_ref, factors_hbm, sem)
    copy.start()
    high, low = padded(columns), padded(columns) + padded(row_count)
    upper_high = -0.5 * message_ref[:, high : high + row_count].astype(jnp.float32)
    upper_low = -0.5 * message_ref[:, low : low + row_count].astype(jnp.float32)
    lower_high, lower_low = split(0.5 * lower_basis_ref[...])
    factor_high, factor_low = split(upper)
    products_high, products_low = split(-lower_products_ref[...])
    for mat in range(mats):
        rows = slice(mat * rank, (mat + 1) * rank)
        lefts = [upper_high, upper_low, upper_high, lower_high, lower_low, lower_high, lower_high, lower_low]
        left_ref[mat] = jnp.concatenate([part[rows] for part in lefts], 0).T.astype(jnp.bfloat16)
        rights = [factor_high, factor_high, factor_low, products_high, products_high, products_low]
        right_ref[mat] = jnp.concatenate([part[rows] for part in rights], 0).astype(jnp.bfloat16)
    copy.wait()


def update_kernel(left_ref, right_ref, odd_ref, even_ref, window_ref, updated_ref, held_ref, sems):
    mats, _, columns = window_ref.shape
    rank = odd_ref.shape[0] // mats
    width = 2 * LANES
    odd = odd_replica()
    copies = []
    for mat in range(mats):
        rows = slice(mat * rank, (mat + 1) * rank)
        for start in range(0, columns, width):
            stop = min(start + width, columns)
            lower = jnp.where(
                odd, even_ref[:, start:stop].astype(jnp.float32), odd_ref[:, start:stop].astype(jnp.float32)
            )[rows]
            last = jnp.concatenate([lower, lower], 0).astype(jnp.bfloat16)
            right = jnp.concatenate([right_ref[mat, :, start:stop], last], 0)
            change = jnp.dot(left_ref[mat], right, preferred_element_type=jnp.float32)
            held_ref[mat, :, start:stop] = (window_ref[mat, :, start:stop].astype(jnp.float32) + change).astype(
                jnp.bfloat16
            )
        copies.append(pltpu.make_async_copy(held_ref.at[mat], updated_ref.at[mat, 0], sems.at[mat]))
        copies[-1].start()
    for copy in copies:
        copy.wait()


def call(kernel, outs, flops, in_specs=None, out_specs=None, **more):
    def run(*operands):
        return pl.pallas_call(
            kernel,
            out_shape=outs,
            in_specs=[IN_VMEM] * len(operands) if in_specs is None else in_specs,
            out_specs=jax.tree.map(lambda _: IN_VMEM, outs) if out_specs is None else out_specs,
            cost_estimate=pl.CostEstimate(flops=flops, bytes_accessed=1 << 20, transcendentals=0),
            compiler_params=pltpu.CompilerParams(vmem_limit_bytes=24 << 20),
            **more,
        )(*operands)

    return run


def shards(weights, vectors):
    window = weights[:, 0]
    own_vectors = vectors[:, 0]
    mats, rank, columns = own_vectors.shape
    row_count = window.shape[1]
    stacked = mats * rank
    flops = 2 * stacked * row_count * columns

    def whole(dtype, *dims):
        return jax.ShapeDtypeStruct(dims, dtype)

    f32, bf16 = jnp.float32, jnp.bfloat16
    images = whole(f32, stacked, row_count)
    rounded_images = whole(bf16, stacked, row_count)
    products = whole(f32, stacked, columns)
    rounded_products = whole(bf16, stacked, columns)

    vectors_b = call(
        round_kernel,
        rounded_products,
        100 * flops,
        in_specs=[pl.BlockSpec(memory_space=pltpu.HBM)],
        scratch_shapes=[pltpu.VMEM(own_vectors.shape, f32), pltpu.SemaphoreType.DMA],
    )(pltpu.with_memory_space_constraint(own_vectors, pltpu.HBM))
    odd_up, even_up = parity_shifts("replica", 1)
    odd_down, _ = parity_shifts("replica", -1)
    base = padded(columns)
    odd_vectors = odd_up(vectors_b)
    own_images, message = call(
        own_images_kernel, (images, whole(bf16, stacked, base + 2 * padded(row_count) + row_count)), 400 * flops
    )(vectors_b, window)
    odd_left = odd_up(own_images)
    even_message = even_up(message)
    odd_images = call(odd_images_kernel, images, 400 * flops)(odd_vectors, window)
    differences = call(differences_kernel, images, flops)(even_message, odd_left, odd_images, window)
    group = lax.axis_size("tensor")
    parts = lax.all_to_all(
        jnp.broadcast_to(differences[None], (group, stacked, row_count)), "tensor", 0, 0
    )
    message_out = whole(bf16, stacked, base + padded(row_count) + row_count)
    lower_basis, basis, lower_products, message = call(
        basis_kernel,
        (images, whole(bf16, stacked, padded(row_count) + row_count), products, message_out),
        flops,
    )(parts, window)
    products_outs = (products, rounded_products)

    odd_basis = odd_down(basis)
    lower_products, message = call(
        odd_products_kernel, (products, message_out), 400 * flops, input_output_aliases={2: 0, 3: 1}
    )(basis, window, lower_products, message)
    message = shifted(message, "replica", -1)
    odd_upper, rounded_upper = call(functools.partial(upper_products_kernel, True, 0), products_outs, 400 * flops)(
        odd_basis, window
    )
    odd_previous = odd_up(rounded_upper)
    even_upper, rounded_upper = call(functools.partial(upper_products_kernel, False, base), products_outs, 0)(
        message, window
    )
    even_previous = even_up(rounded_upper)
    left, right, factors = call(
        factors_kernel,
        (
            whole(bf16, mats, row_count, 8 * rank),
            whole(bf16, mats, 6 * rank, columns),
            whole(f32, mats, 1, rank, columns),
        ),
        flops // 4,
        out_specs=(IN_VMEM, IN_VMEM, pl.BlockSpec(memory_space=pl.ANY)),
        scratch_shapes=[pltpu.VMEM((mats, 1, rank, columns), f32), pltpu.SemaphoreType.DMA],
    )(message, odd_upper, even_upper, lower_basis, lower_products)
    updated = call(
        update_kernel,
        whole(bf16, mats, 1, row_count, columns),
        4 * flops,
        out_specs=pl.BlockSpec(memory_space=pl.ANY),
        scratch_shapes=[pltpu.VMEM((mats, row_count, columns), bf16), pltpu.SemaphoreType.DMA((mats,))],
    )(left, right, odd_previous, even_previous, window)
    return (updated, factors)


def solution(mesh):
    placed = (P(None, "replica", None, "tensor"), P(None, "replica", None, "tensor"))
    return jax.shard_map(
        shards,
        mesh=mesh,
        in_specs=placed,
        out_specs=(P(None, "replica", None, "tensor"), P(None, "replica", None, "tensor")),
        check_vma=False,
    )
```

```python
import functools

import jax
import jax.numpy as jnp
from jax import lax
from jax.experimental import pallas as pl
from jax.experimental.pallas import tpu as pltpu
from jax.sharding import PartitionSpec as P

LANES = 128
ROWS_BY_ROWS = (((1,), (1,)), ((), ()))
IN_VMEM = pl.BlockSpec(memory_space=pltpu.VMEM)


def shifted(value, axis, steps):
    count = lax.axis_size(axis)
    return lax.ppermute(value, axis, [(source, (source + steps) % count) for source in range(count)])


def parity_shifts(axis, steps):
    count = lax.axis_size(axis)

    def over(parity):
        pairs = [
            (source, (source + steps) % count)
            for source in range(count)
            if (source + min(steps, 0)) % 2 == parity
        ]
        return lambda value: lax.ppermute(value, axis, pairs)

    return over(1), over(0)


def padded(size):
    return -(-size // LANES) * LANES


def odd_replica():
    return lax.rem(lax.axis_index("replica"), 2) == 1


def images_of(vectors, window_ref, mat):
    return lax.dot_general(
        vectors.astype(jnp.bfloat16), window_ref[mat], ROWS_BY_ROWS, preferred_element_type=jnp.float32
    )


def own_images_kernel(vectors_ref, window_ref, images_ref, message_ref):
    mats, row_count, columns = window_ref.shape
    rank = images_ref.shape[0] // mats
    vectors = vectors_ref[...].astype(jnp.float32)
    images = jnp.concatenate(
        [images_of(vectors[mat * rank : (mat + 1) * rank], window_ref, mat) for mat in range(mats)], 0
    )
    images_ref[...] = images

    @pl.when(jnp.logical_not(odd_replica()))
    def _():
        message_ref[:, :columns] = vectors_ref[...]
        rest = images
        for part in range(3):
            start = padded(columns) + part * padded(row_count)
            high, rest = split(rest)
            message_ref[:, start : start + row_count] = high.astype(jnp.bfloat16)


def odd_images_kernel(vectors_ref, window_ref, images_ref):
    mats = window_ref.shape[0]
    rank = images_ref.shape[0] // mats

    @pl.when(jnp.logical_not(odd_replica()))
    def _():
        vectors = vectors_ref[...].astype(jnp.float32)
        for mat in range(mats):
            rows = slice(mat * rank, (mat + 1) * rank)
            images_ref[rows] = images_of(vectors[rows], window_ref, mat)


def differences_kernel(even_message_ref, odd_left_ref, odd_images_ref, window_ref, differences_ref):
    mats, row_count, columns = window_ref.shape
    rank = odd_images_ref.shape[0] // mats

    @pl.when(odd_replica())
    def _():
        starts = [padded(columns) + part * padded(row_count) for part in range(3)]
        high, middle, low = (
            even_message_ref[:, start : start + row_count].astype(jnp.float32) for start in starts
        )
        left_images = high + (middle + low)
        vectors = even_message_ref[:, :columns].astype(jnp.float32)
        for mat in range(mats):
            rows = slice(mat * rank, (mat + 1) * rank)
            differences_ref[rows] = left_images[rows] - images_of(vectors[rows], window_ref, mat)

    @pl.when(jnp.logical_not(odd_replica()))
    def _():
        differences_ref[...] = odd_left_ref[...] - odd_images_ref[...]


def round_kernel(vectors_hbm, rounded_ref, held_ref, sem):
    copy = pltpu.make_async_copy(vectors_hbm, held_ref, sem)
    copy.start()
    copy.wait()
    mats = held_ref.shape[0]
    rounded_ref[...] = jnp.concatenate([held_ref[mat] for mat in range(mats)], 0).astype(jnp.bfloat16)


def orthonormal_rows(gram, images, rank):
    mats = gram.shape[0] // rank
    count = images.shape[1]

    def column(mat, step):
        at = mat * rank + step
        return jnp.broadcast_to(gram[mat * rank : (mat + 1) * rank, at : at + 1], (rank, LANES))

    def widened(value):
        return jnp.concatenate([value] * (padded(count) // LANES), 1)[:, :count]

    place = lax.broadcasted_iota(jnp.int32, (rank, LANES), 0)
    columns = [[column(mat, step) for step in range(rank)] for mat in range(mats)]
    rows = [images[mat * rank : (mat + 1) * rank] for mat in range(mats)]
    pivots = [jnp.ones((rank, LANES), jnp.float32) for _ in range(mats)]
    for step in range(rank):
        for mat in range(mats):
            pivot = columns[mat][step][step : step + 1]
            pivots[mat] = jnp.where(place == step, pivot, pivots[mat])
            factor = jnp.where(place > step, columns[mat][step] / pivot, 0.0)
            for later in range(step + 1, rank):
                columns[mat][later] = columns[mat][later] - factor * columns[mat][later][step : step + 1]
            if step < rank - 1:
                rows[mat] = rows[mat] - widened(factor) * rows[mat][step : step + 1]
    return jnp.concatenate([row / widened(jnp.sqrt(pivot)) for row, pivot in zip(rows, pivots)], 0)


def split(value):
    high = value.astype(jnp.bfloat16).astype(jnp.float32)
    return high, value - high


def products_into(basis_ref, window_ref, products_ref, rounded_ref):
    mats, row_count, _ = window_ref.shape
    rank = products_ref.shape[0] // mats
    basis = basis_ref[:, :row_count].astype(jnp.float32)
    for mat in range(mats):
        rows = slice(mat * rank, (mat + 1) * rank)
        products_ref[rows] = jnp.dot(
            basis[rows].astype(jnp.bfloat16), window_ref[mat], preferred_element_type=jnp.float32
        )
    rounded_ref[...] = products_ref[...].astype(jnp.bfloat16)


def lower_products(basis_ref, window_ref, products_ref, message_ref):
    columns = products_ref.shape[1]
    products_into(basis_ref, window_ref, products_ref, message_ref.at[:, :columns])
    message_ref[:, padded(columns) :] = basis_ref[...]


def basis_and_products(parts_ref, window_ref, basis_ref, split_ref, products_ref, message_ref):
    rank = parts_ref.shape[1] // window_ref.shape[0]
    row_count = parts_ref.shape[2]
    images = jnp.sum(parts_ref[...], 0)
    gram = lax.dot_general(
        images, images, ROWS_BY_ROWS, precision=lax.Precision.HIGHEST, preferred_element_type=jnp.float32
    )
    basis = orthonormal_rows(gram, images, rank)
    basis_ref[...] = basis
    high, low = split(basis)
    split_ref[:, :row_count] = high.astype(jnp.bfloat16)
    start = padded(row_count)
    split_ref[:, start : start + row_count] = low.astype(jnp.bfloat16)
    lower_products(split_ref, window_ref, products_ref, message_ref)


def even_basis_kernel(parts_ref, window_ref, basis_ref, split_ref, products_ref, message_ref):
    @pl.when(jnp.logical_not(odd_replica()))
    def _():
        basis_and_products(parts_ref, window_ref, basis_ref, split_ref, products_ref, message_ref)


def odd_basis_kernel(parts_ref, window_ref, _, __, ___, basis_ref, products_ref, message_ref, split_ref):
    @pl.when(odd_replica())
    def _():
        basis_and_products(parts_ref, window_ref, basis_ref, split_ref, products_ref, message_ref)


def upper_products_kernel(odd, start, message_ref, window_ref, products_ref, rounded_ref):
    @pl.when(odd_replica() == odd)
    def _():
        products_into(message_ref.at[:, start:], window_ref, products_ref, rounded_ref)


def factors_kernel(
    message_ref,
    odd_products_ref,
    even_products_ref,
    lower_basis_ref,
    lower_products_ref,
    left_ref,
    right_ref,
    factors_hbm,
    factors_ref,
    sem,
):
    mats, row_count, _ = left_ref.shape
    stacked, columns = lower_products_ref.shape
    rank = stacked // mats
    upper = jnp.where(odd_replica(), odd_products_ref[...], even_products_ref[...]) - message_ref[
        :, :columns
    ].astype(jnp.float32)
    for mat in range(mats):
        factors_ref[mat, 0] = upper[mat * rank : (mat + 1) * rank]
    copy = pltpu.make_async_copy(factors_ref, factors_hbm, sem)
    copy.start()
    high, low = padded(columns), padded(columns) + padded(row_count)
    upper_high = -0.5 * message_ref[:, high : high + row_count].astype(jnp.float32)
    upper_low = -0.5 * message_ref[:, low : low + row_count].astype(jnp.float32)
    lower_high, lower_low = split(0.5 * lower_basis_ref[...])
    factor_high, factor_low = split(upper)
    products_high, products_low = split(-lower_products_ref[...])
    for mat in range(mats):
        rows = slice(mat * rank, (mat + 1) * rank)
        lefts = [upper_high, upper_low, upper_high, lower_high, lower_low, lower_high, lower_high, lower_low]
        left_ref[mat] = jnp.concatenate([part[rows] for part in lefts], 0).T.astype(jnp.bfloat16)
        rights = [factor_high, factor_high, factor_low, products_high, products_high, products_low]
        right_ref[mat] = jnp.concatenate([part[rows] for part in rights], 0).astype(jnp.bfloat16)
    copy.wait()


def update_kernel(left_ref, right_ref, odd_ref, even_ref, window_ref, updated_ref, held_ref, sems):
    mats, _, columns = window_ref.shape
    rank = odd_ref.shape[0] // mats
    width = 2 * LANES
    odd = odd_replica()
    copies = []
    for mat in range(mats):
        rows = slice(mat * rank, (mat + 1) * rank)
        for start in range(0, columns, width):
            stop = min(start + width, columns)
            lower = jnp.where(
                odd, even_ref[:, start:stop].astype(jnp.float32), odd_ref[:, start:stop].astype(jnp.float32)
            )[rows]
            last = jnp.concatenate([lower, lower], 0).astype(jnp.bfloat16)
            right = jnp.concatenate([right_ref[mat, :, start:stop], last], 0)
            change = jnp.dot(left_ref[mat], right, preferred_element_type=jnp.float32)
            held_ref[mat, :, start:stop] = (window_ref[mat, :, start:stop].astype(jnp.float32) + change).astype(
                jnp.bfloat16
            )
        copies.append(pltpu.make_async_copy(held_ref.at[mat], updated_ref.at[mat, 0], sems.at[mat]))
        copies[-1].start()
    for copy in copies:
        copy.wait()


def call(kernel, outs, flops, in_specs=None, out_specs=None, **more):
    def run(*operands):
        return pl.pallas_call(
            kernel,
            out_shape=outs,
            in_specs=[IN_VMEM] * len(operands) if in_specs is None else in_specs,
            out_specs=jax.tree.map(lambda _: IN_VMEM, outs) if out_specs is None else out_specs,
            cost_estimate=pl.CostEstimate(flops=flops, bytes_accessed=1 << 20, transcendentals=0),
            compiler_params=pltpu.CompilerParams(vmem_limit_bytes=24 << 20),
            **more,
        )(*operands)

    return run


def shards(weights, vectors):
    window = weights[:, 0]
    own_vectors = vectors[:, 0]
    mats, rank, columns = own_vectors.shape
    row_count = window.shape[1]
    stacked = mats * rank
    flops = 2 * stacked * row_count * columns

    def whole(dtype, *dims):
        return jax.ShapeDtypeStruct(dims, dtype)

    f32, bf16 = jnp.float32, jnp.bfloat16
    images = whole(f32, stacked, row_count)
    rounded_images = whole(bf16, stacked, row_count)
    products = whole(f32, stacked, columns)
    rounded_products = whole(bf16, stacked, columns)

    vectors_b = call(
        round_kernel,
        rounded_products,
        100 * flops,
        in_specs=[pl.BlockSpec(memory_space=pltpu.HBM)],
        scratch_shapes=[pltpu.VMEM(own_vectors.shape, f32), pltpu.SemaphoreType.DMA],
    )(pltpu.with_memory_space_constraint(own_vectors, pltpu.HBM))
    odd_up, even_up = parity_shifts("replica", 1)
    odd_down, _ = parity_shifts("replica", -1)
    base = padded(columns)
    odd_vectors = odd_up(vectors_b)
    own_images, message = call(
        own_images_kernel, (images, whole(bf16, stacked, base + 2 * padded(row_count) + row_count)), 400 * flops
    )(vectors_b, window)
    odd_left = odd_up(own_images)
    even_message = even_up(message)
    odd_images = call(odd_images_kernel, images, 400 * flops)(odd_vectors, window)
    differences = call(differences_kernel, images, flops)(even_message, odd_left, odd_images, window)
    group = lax.axis_size("tensor")
    parts = lax.all_to_all(
        jnp.broadcast_to(differences[None], (group, stacked, row_count)), "tensor", 0, 0
    )
    message_out = whole(bf16, stacked, base + padded(row_count) + row_count)
    split_basis = whole(bf16, stacked, padded(row_count) + row_count)
    lower_basis, basis, lower_products, message = call(
        even_basis_kernel, (images, split_basis, products, message_out), flops
    )(parts, window)
    products_outs = (products, rounded_products)

    odd_basis = odd_down(basis)
    lower_basis, lower_products, message = call(
        odd_basis_kernel,
        (images, products, message_out),
        400 * flops,
        input_output_aliases={2: 0, 3: 1, 4: 2},
        scratch_shapes=[pltpu.VMEM(split_basis.shape, bf16)],
    )(parts, window, lower_basis, lower_products, message)
    message = shifted(message, "replica", -1)
    odd_upper, rounded_upper = call(functools.partial(upper_products_kernel, True, 0), products_outs, 400 * flops)(
        odd_basis, window
    )
    odd_previous = odd_up(rounded_upper)
    even_upper, rounded_upper = call(functools.partial(upper_products_kernel, False, base), products_outs, 0)(
        message, window
    )
    even_previous = even_up(rounded_upper)
    left, right, factors = call(
        factors_kernel,
        (
            whole(bf16, mats, row_count, 8 * rank),
            whole(bf16, mats, 6 * rank, columns),
            whole(f32, mats, 1, rank, columns),
        ),
        flops // 4,
        out_specs=(IN_VMEM, IN_VMEM, pl.BlockSpec(memory_space=pl.ANY)),
        scratch_shapes=[pltpu.VMEM((mats, 1, rank, columns), f32), pltpu.SemaphoreType.DMA],
    )(message, odd_upper, even_upper, lower_basis, lower_products)
    updated = call(
        update_kernel,
        whole(bf16, mats, 1, row_count, columns),
        4 * flops,
        out_specs=pl.BlockSpec(memory_space=pl.ANY),
        scratch_shapes=[pltpu.VMEM((mats, row_count, columns), bf16), pltpu.SemaphoreType.DMA((mats,))],
    )(left, right, odd_previous, even_previous, window)
    return (updated, factors)


def solution(mesh):
    placed = (P(None, "replica", None, "tensor"), P(None, "replica", None, "tensor"))
    return jax.shard_map(
        shards,
        mesh=mesh,
        in_specs=placed,
        out_specs=(P(None, "replica", None, "tensor"), P(None, "replica", None, "tensor")),
        check_vma=False,
    )
```

```python
import functools

import jax
import jax.numpy as jnp
from jax import lax
from jax.experimental import pallas as pl
from jax.experimental.pallas import tpu as pltpu
from jax.sharding import PartitionSpec as P

LANES = 128
ROWS_BY_ROWS = (((1,), (1,)), ((), ()))
IN_VMEM = pl.BlockSpec(memory_space=pltpu.VMEM)


def shifted(value, axis, steps):
    count = lax.axis_size(axis)
    return lax.ppermute(value, axis, [(source, (source + steps) % count) for source in range(count)])


def parity_shifts(axis, steps):
    count = lax.axis_size(axis)

    def over(parity):
        pairs = [
            (source, (source + steps) % count)
            for source in range(count)
            if (source + min(steps, 0)) % 2 == parity
        ]
        return lambda value: lax.ppermute(value, axis, pairs)

    return over(1), over(0)


def padded(size):
    return -(-size // LANES) * LANES


def odd_replica():
    return lax.rem(lax.axis_index("replica"), 2) == 1


def images_of(vectors, window_ref, mat):
    return lax.dot_general(
        vectors.astype(jnp.bfloat16), window_ref[mat], ROWS_BY_ROWS, preferred_element_type=jnp.float32
    )


def own_images_kernel(vectors_ref, window_ref, images_ref, message_ref):
    mats, row_count, columns = window_ref.shape
    rank = images_ref.shape[0] // mats
    vectors = vectors_ref[...].astype(jnp.float32)
    images = jnp.concatenate(
        [images_of(vectors[mat * rank : (mat + 1) * rank], window_ref, mat) for mat in range(mats)], 0
    )
    images_ref[...] = images

    @pl.when(jnp.logical_not(odd_replica()))
    def _():
        message_ref[:, :columns] = vectors_ref[...]
        rest = images
        for part in range(3):
            start = padded(columns) + part * padded(row_count)
            high, rest = split(rest)
            message_ref[:, start : start + row_count] = high.astype(jnp.bfloat16)


def odd_images_kernel(vectors_ref, window_ref, images_ref):
    mats = window_ref.shape[0]
    rank = images_ref.shape[0] // mats

    @pl.when(jnp.logical_not(odd_replica()))
    def _():
        vectors = vectors_ref[...].astype(jnp.float32)
        for mat in range(mats):
            rows = slice(mat * rank, (mat + 1) * rank)
            images_ref[rows] = images_of(vectors[rows], window_ref, mat)


def differences_kernel(even_message_ref, odd_left_ref, odd_images_ref, window_ref, differences_ref):
    mats, row_count, columns = window_ref.shape
    rank = odd_images_ref.shape[0] // mats

    @pl.when(odd_replica())
    def _():
        starts = [padded(columns) + part * padded(row_count) for part in range(3)]
        high, middle, low = (
            even_message_ref[:, start : start + row_count].astype(jnp.float32) for start in starts
        )
        left_images = high + (middle + low)
        vectors = even_message_ref[:, :columns].astype(jnp.float32)
        for mat in range(mats):
            rows = slice(mat * rank, (mat + 1) * rank)
            differences_ref[rows] = left_images[rows] - images_of(vectors[rows], window_ref, mat)

    @pl.when(jnp.logical_not(odd_replica()))
    def _():
        differences_ref[...] = odd_left_ref[...] - odd_images_ref[...]


def round_kernel(vectors_hbm, rounded_ref, held_ref, sem):
    copy = pltpu.make_async_copy(vectors_hbm, held_ref, sem)
    copy.start()
    copy.wait()
    mats = held_ref.shape[0]
    rounded_ref[...] = jnp.concatenate([held_ref[mat] for mat in range(mats)], 0).astype(jnp.bfloat16)


def orthonormal_rows(gram, images, rank):
    mats = gram.shape[0] // rank
    count = images.shape[1]

    def column(mat, step):
        at = mat * rank + step
        return jnp.broadcast_to(gram[mat * rank : (mat + 1) * rank, at : at + 1], (rank, LANES))

    def widened(value):
        return jnp.concatenate([value] * (padded(count) // LANES), 1)[:, :count]

    place = lax.broadcasted_iota(jnp.int32, (rank, LANES), 0)
    columns = [[column(mat, step) for step in range(rank)] for mat in range(mats)]
    rows = [images[mat * rank : (mat + 1) * rank] for mat in range(mats)]
    pivots = [jnp.ones((rank, LANES), jnp.float32) for _ in range(mats)]
    for step in range(rank):
        for mat in range(mats):
            pivot = columns[mat][step][step : step + 1]
            pivots[mat] = jnp.where(place == step, pivot, pivots[mat])
            factor = jnp.where(place > step, columns[mat][step] / pivot, 0.0)
            for later in range(step + 1, rank):
                columns[mat][later] = columns[mat][later] - factor * columns[mat][later][step : step + 1]
            if step < rank - 1:
                rows[mat] = rows[mat] - widened(factor) * rows[mat][step : step + 1]
    return jnp.concatenate([row / widened(jnp.sqrt(pivot)) for row, pivot in zip(rows, pivots)], 0)


def split(value):
    high = value.astype(jnp.bfloat16).astype(jnp.float32)
    return high, value - high


def products_into(basis_ref, window_ref, products_ref, rounded_ref):
    mats, row_count, _ = window_ref.shape
    rank = products_ref.shape[0] // mats
    basis = basis_ref[:, :row_count].astype(jnp.float32)
    for mat in range(mats):
        rows = slice(mat * rank, (mat + 1) * rank)
        products_ref[rows] = jnp.dot(
            basis[rows].astype(jnp.bfloat16), window_ref[mat], preferred_element_type=jnp.float32
        )
    rounded_ref[...] = products_ref[...].astype(jnp.bfloat16)


def lower_products(basis_ref, window_ref, products_ref, message_ref):
    columns = products_ref.shape[1]
    products_into(basis_ref, window_ref, products_ref, message_ref.at[:, :columns])
    message_ref[:, padded(columns) :] = basis_ref[...]


def basis_and_products(parts_ref, window_ref, basis_ref, split_ref, products_ref, message_ref):
    rank = parts_ref.shape[1] // window_ref.shape[0]
    row_count = parts_ref.shape[2]
    images = jnp.sum(parts_ref[...], 0)
    gram = lax.dot_general(
        images, images, ROWS_BY_ROWS, precision=lax.Precision.HIGHEST, preferred_element_type=jnp.float32
    )
    basis = orthonormal_rows(gram, images, rank)
    basis_ref[...] = basis
    high, low = split(basis)
    split_ref[:, :row_count] = high.astype(jnp.bfloat16)
    start = padded(row_count)
    split_ref[:, start : start + row_count] = low.astype(jnp.bfloat16)
    lower_products(split_ref, window_ref, products_ref, message_ref)


def even_basis_kernel(parts_ref, window_ref, basis_ref, split_ref, products_ref, message_ref):
    @pl.when(jnp.logical_not(odd_replica()))
    def _():
        basis_and_products(parts_ref, window_ref, basis_ref, split_ref, products_ref, message_ref)


def odd_basis_kernel(parts_ref, window_ref, _, __, ___, basis_ref, products_ref, message_ref, split_ref):
    @pl.when(odd_replica())
    def _():
        basis_and_products(parts_ref, window_ref, basis_ref, split_ref, products_ref, message_ref)


def upper_products_kernel(odd, start, message_ref, window_ref, products_ref, rounded_ref):
    @pl.when(odd_replica() == odd)
    def _():
        products_into(message_ref.at[:, start:], window_ref, products_ref, rounded_ref)


def factors_kernel(
    message_ref,
    odd_products_ref,
    even_products_ref,
    lower_basis_ref,
    lower_products_ref,
    left_ref,
    right_ref,
    factors_hbm,
    factors_ref,
    sem,
):
    mats, row_count, _ = left_ref.shape
    stacked, columns = lower_products_ref.shape
    rank = stacked // mats
    upper = jnp.where(odd_replica(), odd_products_ref[...], even_products_ref[...]) - message_ref[
        :, :columns
    ].astype(jnp.float32)
    for mat in range(mats):
        factors_ref[mat, 0] = upper[mat * rank : (mat + 1) * rank]
    copy = pltpu.make_async_copy(factors_ref, factors_hbm, sem)
    copy.start()
    high, low = padded(columns), padded(columns) + padded(row_count)
    upper_high = -0.5 * message_ref[:, high : high + row_count].astype(jnp.float32)
    upper_low = -0.5 * message_ref[:, low : low + row_count].astype(jnp.float32)
    lower_high, lower_low = split(0.5 * lower_basis_ref[...])
    factor_high, factor_low = split(upper)
    products_high, products_low = split(-lower_products_ref[...])
    for mat in range(mats):
        rows = slice(mat * rank, (mat + 1) * rank)
        lefts = [upper_high, upper_low, upper_high, lower_high, lower_low, lower_high, lower_high, lower_low]
        left_ref[mat] = jnp.concatenate([part[rows] for part in lefts], 0).T.astype(jnp.bfloat16)
        rights = [factor_high, factor_high, factor_low, products_high, products_high, products_low]
        right_ref[mat] = jnp.concatenate([part[rows] for part in rights], 0).astype(jnp.bfloat16)
    copy.wait()


def update_kernel(left_ref, right_ref, odd_ref, even_ref, window_ref, updated_ref, held_ref, sems):
    mats, _, columns = window_ref.shape
    rank = odd_ref.shape[0] // mats
    width = 2 * LANES
    odd = odd_replica()
    copies = []
    for mat in range(mats):
        rows = slice(mat * rank, (mat + 1) * rank)
        for start in range(0, columns, width):
            stop = min(start + width, columns)
            lower = jnp.where(
                odd, even_ref[:, start:stop].astype(jnp.float32), odd_ref[:, start:stop].astype(jnp.float32)
            )[rows]
            last = jnp.concatenate([lower, lower], 0).astype(jnp.bfloat16)
            right = jnp.concatenate([right_ref[mat, :, start:stop], last], 0)
            change = jnp.dot(left_ref[mat], right, preferred_element_type=jnp.float32)
            held_ref[mat, :, start:stop] = (window_ref[mat, :, start:stop].astype(jnp.float32) + change).astype(
                jnp.bfloat16
            )
            if stop % (2 * width) == 0 or stop == columns:
                piece = slice(start // (2 * width) * (2 * width), stop)
                copies.append(
                    pltpu.make_async_copy(
                        held_ref.at[mat, :, piece], updated_ref.at[mat, 0, :, piece], sems.at[len(copies)]
                    )
                )
                copies[-1].start()
    for copy in copies:
        copy.wait()


def call(kernel, outs, flops, in_specs=None, out_specs=None, **more):
    def run(*operands):
        return pl.pallas_call(
            kernel,
            out_shape=outs,
            in_specs=[IN_VMEM] * len(operands) if in_specs is None else in_specs,
            out_specs=jax.tree.map(lambda _: IN_VMEM, outs) if out_specs is None else out_specs,
            cost_estimate=pl.CostEstimate(flops=flops, bytes_accessed=1 << 20, transcendentals=0),
            compiler_params=pltpu.CompilerParams(vmem_limit_bytes=24 << 20),
            **more,
        )(*operands)

    return run


def shards(weights, vectors):
    window = weights[:, 0]
    own_vectors = vectors[:, 0]
    mats, rank, columns = own_vectors.shape
    row_count = window.shape[1]
    stacked = mats * rank
    flops = 2 * stacked * row_count * columns

    def whole(dtype, *dims):
        return jax.ShapeDtypeStruct(dims, dtype)

    f32, bf16 = jnp.float32, jnp.bfloat16
    images = whole(f32, stacked, row_count)
    rounded_images = whole(bf16, stacked, row_count)
    products = whole(f32, stacked, columns)
    rounded_products = whole(bf16, stacked, columns)

    vectors_b = call(
        round_kernel,
        rounded_products,
        100 * flops,
        in_specs=[pl.BlockSpec(memory_space=pltpu.HBM)],
        scratch_shapes=[pltpu.VMEM(own_vectors.shape, f32), pltpu.SemaphoreType.DMA],
    )(pltpu.with_memory_space_constraint(own_vectors, pltpu.HBM))
    odd_up, even_up = parity_shifts("replica", 1)
    odd_down, _ = parity_shifts("replica", -1)
    base = padded(columns)
    odd_vectors = odd_up(vectors_b)
    own_images, message = call(
        own_images_kernel, (images, whole(bf16, stacked, base + 2 * padded(row_count) + row_count)), 400 * flops
    )(vectors_b, window)
    odd_left = odd_up(own_images)
    even_message = even_up(message)
    odd_images = call(odd_images_kernel, images, 400 * flops)(odd_vectors, window)
    differences = call(differences_kernel, images, flops)(even_message, odd_left, odd_images, window)
    group = lax.axis_size("tensor")
    parts = lax.all_to_all(
        jnp.broadcast_to(differences[None], (group, stacked, row_count)), "tensor", 0, 0
    )
    message_out = whole(bf16, stacked, base + padded(row_count) + row_count)
    split_basis = whole(bf16, stacked, padded(row_count) + row_count)
    lower_basis, basis, lower_products, message = call(
        even_basis_kernel, (images, split_basis, products, message_out), flops
    )(parts, window)
    products_outs = (products, rounded_products)

    odd_basis = odd_down(basis)
    lower_basis, lower_products, message = call(
        odd_basis_kernel,
        (images, products, message_out),
        400 * flops,
        input_output_aliases={2: 0, 3: 1, 4: 2},
        scratch_shapes=[pltpu.VMEM(split_basis.shape, bf16)],
    )(parts, window, lower_basis, lower_products, message)
    message = shifted(message, "replica", -1)
    odd_upper, rounded_upper = call(functools.partial(upper_products_kernel, True, 0), products_outs, 400 * flops)(
        odd_basis, window
    )
    odd_previous = odd_up(rounded_upper)
    even_upper, rounded_upper = call(functools.partial(upper_products_kernel, False, base), products_outs, 0)(
        message, window
    )
    even_previous = even_up(rounded_upper)
    left, right, factors = call(
        factors_kernel,
        (
            whole(bf16, mats, row_count, 8 * rank),
            whole(bf16, mats, 6 * rank, columns),
            whole(f32, mats, 1, rank, columns),
        ),
        flops // 4,
        out_specs=(IN_VMEM, IN_VMEM, pl.BlockSpec(memory_space=pl.ANY)),
        scratch_shapes=[pltpu.VMEM((mats, 1, rank, columns), f32), pltpu.SemaphoreType.DMA],
    )(message, odd_upper, even_upper, lower_basis, lower_products)
    updated = call(
        update_kernel,
        whole(bf16, mats, 1, row_count, columns),
        4 * flops,
        out_specs=pl.BlockSpec(memory_space=pl.ANY),
        scratch_shapes=[pltpu.VMEM((mats, row_count, columns), bf16), pltpu.SemaphoreType.DMA((mats * (-(-columns // (4 * LANES))),))],
    )(left, right, odd_previous, even_previous, window)
    return (updated, factors)


def solution(mesh):
    placed = (P(None, "replica", None, "tensor"), P(None, "replica", None, "tensor"))
    return jax.shard_map(
        shards,
        mesh=mesh,
        in_specs=placed,
        out_specs=(P(None, "replica", None, "tensor"), P(None, "replica", None, "tensor")),
        check_vma=False,
    )
```

```python
import functools

import jax
import jax.numpy as jnp
from jax import lax
from jax.experimental import pallas as pl
from jax.experimental.pallas import tpu as pltpu
from jax.sharding import PartitionSpec as P

LANES = 128
ROWS_BY_ROWS = (((1,), (1,)), ((), ()))
IN_VMEM = pl.BlockSpec(memory_space=pltpu.VMEM)


def shifted(value, axis, steps):
    count = lax.axis_size(axis)
    return lax.ppermute(value, axis, [(source, (source + steps) % count) for source in range(count)])


def parity_shifts(axis, steps):
    count = lax.axis_size(axis)

    def over(parity):
        pairs = [
            (source, (source + steps) % count)
            for source in range(count)
            if (source + min(steps, 0)) % 2 == parity
        ]
        return lambda value: lax.ppermute(value, axis, pairs)

    return over(1), over(0)


def padded(size):
    return -(-size // LANES) * LANES


def odd_replica():
    return lax.rem(lax.axis_index("replica"), 2) == 1


def images_of(vectors, window_ref, mat):
    return lax.dot_general(
        vectors.astype(jnp.bfloat16), window_ref[mat], ROWS_BY_ROWS, preferred_element_type=jnp.float32
    )


def own_images_kernel(vectors_ref, window_ref, images_ref, message_ref):
    mats, row_count, columns = window_ref.shape
    rank = images_ref.shape[0] // mats
    vectors = vectors_ref[...].astype(jnp.float32)
    images = jnp.concatenate(
        [images_of(vectors[mat * rank : (mat + 1) * rank], window_ref, mat) for mat in range(mats)], 0
    )
    images_ref[...] = images

    @pl.when(jnp.logical_not(odd_replica()))
    def _():
        message_ref[:, :columns] = vectors_ref[...]
        rest = images
        for part in range(3):
            start = padded(columns) + part * padded(row_count)
            high, rest = split(rest)
            message_ref[:, start : start + row_count] = high.astype(jnp.bfloat16)


def odd_images_kernel(vectors_ref, window_ref, images_ref):
    mats = window_ref.shape[0]
    rank = images_ref.shape[0] // mats

    @pl.when(jnp.logical_not(odd_replica()))
    def _():
        vectors = vectors_ref[...].astype(jnp.float32)
        for mat in range(mats):
            rows = slice(mat * rank, (mat + 1) * rank)
            images_ref[rows] = images_of(vectors[rows], window_ref, mat)


def differences_kernel(even_message_ref, odd_left_ref, odd_images_ref, window_ref, differences_ref):
    mats, row_count, columns = window_ref.shape
    rank = odd_images_ref.shape[0] // mats

    @pl.when(odd_replica())
    def _():
        starts = [padded(columns) + part * padded(row_count) for part in range(3)]
        high, middle, low = (
            even_message_ref[:, start : start + row_count].astype(jnp.float32) for start in starts
        )
        left_images = high + (middle + low)
        vectors = even_message_ref[:, :columns].astype(jnp.float32)
        for mat in range(mats):
            rows = slice(mat * rank, (mat + 1) * rank)
            differences_ref[rows] = left_images[rows] - images_of(vectors[rows], window_ref, mat)

    @pl.when(jnp.logical_not(odd_replica()))
    def _():
        differences_ref[...] = odd_left_ref[...] - odd_images_ref[...]


def round_kernel(vectors_hbm, rounded_ref, held_ref, sem):
    copy = pltpu.make_async_copy(vectors_hbm, held_ref, sem)
    copy.start()
    copy.wait()
    mats = held_ref.shape[0]
    rounded_ref[...] = jnp.concatenate([held_ref[mat] for mat in range(mats)], 0).astype(jnp.bfloat16)


def orthonormal_rows(gram, images, rank):
    mats = gram.shape[0] // rank
    count = images.shape[1]

    def column(mat, step):
        at = mat * rank + step
        return jnp.broadcast_to(gram[mat * rank : (mat + 1) * rank, at : at + 1], (rank, LANES))

    def widened(value):
        return jnp.concatenate([value] * (padded(count) // LANES), 1)[:, :count]

    place = lax.broadcasted_iota(jnp.int32, (rank, LANES), 0)
    columns = [[column(mat, step) for step in range(rank)] for mat in range(mats)]
    rows = [images[mat * rank : (mat + 1) * rank] for mat in range(mats)]
    pivots = [jnp.ones((rank, LANES), jnp.float32) for _ in range(mats)]
    for step in range(rank):
        for mat in range(mats):
            pivot = columns[mat][step][step : step + 1]
            pivots[mat] = jnp.where(place == step, pivot, pivots[mat])
            factor = jnp.where(place > step, columns[mat][step] / pivot, 0.0)
            for later in range(step + 1, rank):
                columns[mat][later] = columns[mat][later] - factor * columns[mat][later][step : step + 1]
            if step < rank - 1:
                rows[mat] = rows[mat] - widened(factor) * rows[mat][step : step + 1]
    return jnp.concatenate([row / widened(jnp.sqrt(pivot)) for row, pivot in zip(rows, pivots)], 0)


def split(value):
    high = value.astype(jnp.bfloat16).astype(jnp.float32)
    return high, value - high


def products_into(basis_ref, window_ref, products_ref, rounded_ref):
    mats, row_count, _ = window_ref.shape
    rank = products_ref.shape[0] // mats
    basis = basis_ref[:, :row_count].astype(jnp.float32)
    for mat in range(mats):
        rows = slice(mat * rank, (mat + 1) * rank)
        products_ref[rows] = jnp.dot(
            basis[rows].astype(jnp.bfloat16), window_ref[mat], preferred_element_type=jnp.float32
        )
    rounded_ref[...] = products_ref[...].astype(jnp.bfloat16)


def lower_products(basis_ref, window_ref, products_ref, message_ref):
    columns = products_ref.shape[1]
    products_into(basis_ref, window_ref, products_ref, message_ref.at[:, :columns])
    message_ref[:, padded(columns) :] = basis_ref[...]


def basis_and_products(parts_ref, window_ref, basis_ref, split_ref, products_ref, message_ref):
    rank = parts_ref.shape[1] // window_ref.shape[0]
    row_count = parts_ref.shape[2]
    images = jnp.sum(parts_ref[...], 0)
    gram = lax.dot_general(
        images, images, ROWS_BY_ROWS, precision=lax.Precision.HIGHEST, preferred_element_type=jnp.float32
    )
    basis = orthonormal_rows(gram, images, rank)
    basis_ref[...] = basis
    high, low = split(basis)
    split_ref[:, :row_count] = high.astype(jnp.bfloat16)
    start = padded(row_count)
    split_ref[:, start : start + row_count] = low.astype(jnp.bfloat16)
    lower_products(split_ref, window_ref, products_ref, message_ref)


def even_basis_kernel(parts_ref, window_ref, basis_ref, split_ref, products_ref, message_ref):
    @pl.when(jnp.logical_not(odd_replica()))
    def _():
        basis_and_products(parts_ref, window_ref, basis_ref, split_ref, products_ref, message_ref)


def odd_basis_kernel(parts_ref, window_ref, _, __, ___, basis_ref, products_ref, message_ref, split_ref):
    @pl.when(odd_replica())
    def _():
        basis_and_products(parts_ref, window_ref, basis_ref, split_ref, products_ref, message_ref)


def upper_products_kernel(odd, start, message_ref, window_ref, products_ref, rounded_ref):
    @pl.when(odd_replica() == odd)
    def _():
        products_into(message_ref.at[:, start:], window_ref, products_ref, rounded_ref)


def factors_kernel(
    message_ref,
    odd_products_ref,
    even_products_ref,
    lower_basis_ref,
    lower_products_ref,
    left_ref,
    right_ref,
    factors_hbm,
    factors_ref,
    sem,
):
    mats, row_count, _ = left_ref.shape
    stacked, columns = lower_products_ref.shape
    rank = stacked // mats
    upper = jnp.where(odd_replica(), odd_products_ref[...], even_products_ref[...]) - message_ref[
        :, :columns
    ].astype(jnp.float32)
    for mat in range(mats):
        factors_ref[mat, 0] = upper[mat * rank : (mat + 1) * rank]
    copy = pltpu.make_async_copy(factors_ref, factors_hbm, sem)
    copy.start()
    high, low = padded(columns), padded(columns) + padded(row_count)
    upper_high = -0.5 * message_ref[:, high : high + row_count].astype(jnp.float32)
    upper_low = -0.5 * message_ref[:, low : low + row_count].astype(jnp.float32)
    lower_high, lower_low = split(0.5 * lower_basis_ref[...])
    factor_high, factor_low = split(upper)
    products_high, products_low = split(-lower_products_ref[...])
    for mat in range(mats):
        rows = slice(mat * rank, (mat + 1) * rank)
        lefts = [upper_high, upper_low, upper_high, lower_high, lower_low, lower_high, lower_high, lower_low]
        left_ref[mat] = jnp.concatenate([part[rows] for part in lefts], 0).T.astype(jnp.bfloat16)
        rights = [factor_high, factor_high, factor_low, products_high, products_high, products_low]
        right_ref[mat] = jnp.concatenate([part[rows] for part in rights], 0).astype(jnp.bfloat16)
    copy.wait()


def update_kernel(left_ref, right_ref, odd_ref, even_ref, window_ref, updated_ref, held_ref, sems):
    mats, _, columns = window_ref.shape
    rank = odd_ref.shape[0] // mats
    width = 2 * LANES
    odd = odd_replica()
    copies = []
    for mat in range(mats):
        rows = slice(mat * rank, (mat + 1) * rank)
        for start in range(0, columns, width):
            stop = min(start + width, columns)
            lower = jnp.where(
                odd, even_ref[:, start:stop].astype(jnp.float32), odd_ref[:, start:stop].astype(jnp.float32)
            )[rows]
            last = jnp.concatenate([lower, lower], 0).astype(jnp.bfloat16)
            right = jnp.concatenate([right_ref[mat, :, start:stop], last], 0)
            change = jnp.dot(left_ref[mat], right, preferred_element_type=jnp.float32)
            held_ref[mat, :, start:stop] = (window_ref[mat, :, start:stop].astype(jnp.float32) + change).astype(
                jnp.bfloat16
            )
            if stop % width == 0 or stop == columns:
                piece = slice(start, stop)
                copies.append(
                    pltpu.make_async_copy(
                        held_ref.at[mat, :, piece], updated_ref.at[mat, 0, :, piece], sems.at[len(copies)]
                    )
                )
                copies[-1].start()
    for copy in copies:
        copy.wait()


def call(kernel, outs, flops, in_specs=None, out_specs=None, **more):
    def run(*operands):
        return pl.pallas_call(
            kernel,
            out_shape=outs,
            in_specs=[IN_VMEM] * len(operands) if in_specs is None else in_specs,
            out_specs=jax.tree.map(lambda _: IN_VMEM, outs) if out_specs is None else out_specs,
            cost_estimate=pl.CostEstimate(flops=flops, bytes_accessed=1 << 20, transcendentals=0),
            compiler_params=pltpu.CompilerParams(vmem_limit_bytes=24 << 20),
            **more,
        )(*operands)

    return run


def shards(weights, vectors):
    window = weights[:, 0]
    own_vectors = vectors[:, 0]
    mats, rank, columns = own_vectors.shape
    row_count = window.shape[1]
    stacked = mats * rank
    flops = 2 * stacked * row_count * columns

    def whole(dtype, *dims):
        return jax.ShapeDtypeStruct(dims, dtype)

    f32, bf16 = jnp.float32, jnp.bfloat16
    images = whole(f32, stacked, row_count)
    rounded_images = whole(bf16, stacked, row_count)
    products = whole(f32, stacked, columns)
    rounded_products = whole(bf16, stacked, columns)

    vectors_b = call(
        round_kernel,
        rounded_products,
        100 * flops,
        in_specs=[pl.BlockSpec(memory_space=pltpu.HBM)],
        scratch_shapes=[pltpu.VMEM(own_vectors.shape, f32), pltpu.SemaphoreType.DMA],
    )(pltpu.with_memory_space_constraint(own_vectors, pltpu.HBM))
    odd_up, even_up = parity_shifts("replica", 1)
    odd_down, _ = parity_shifts("replica", -1)
    base = padded(columns)
    odd_vectors = odd_up(vectors_b)
    own_images, message = call(
        own_images_kernel, (images, whole(bf16, stacked, base + 2 * padded(row_count) + row_count)), 400 * flops
    )(vectors_b, window)
    odd_left = odd_up(own_images)
    even_message = even_up(message)
    odd_images = call(odd_images_kernel, images, 400 * flops)(odd_vectors, window)
    differences = call(differences_kernel, images, flops)(even_message, odd_left, odd_images, window)
    group = lax.axis_size("tensor")
    parts = lax.all_to_all(
        jnp.broadcast_to(differences[None], (group, stacked, row_count)), "tensor", 0, 0
    )
    message_out = whole(bf16, stacked, base + padded(row_count) + row_count)
    split_basis = whole(bf16, stacked, padded(row_count) + row_count)
    lower_basis, basis, lower_products, message = call(
        even_basis_kernel, (images, split_basis, products, message_out), flops
    )(parts, window)
    products_outs = (products, rounded_products)

    odd_basis = odd_down(basis)
    lower_basis, lower_products, message = call(
        odd_basis_kernel,
        (images, products, message_out),
        400 * flops,
        input_output_aliases={2: 0, 3: 1, 4: 2},
        scratch_shapes=[pltpu.VMEM(split_basis.shape, bf16)],
    )(parts, window, lower_basis, lower_products, message)
    message = shifted(message, "replica", -1)
    odd_upper, rounded_upper = call(functools.partial(upper_products_kernel, True, 0), products_outs, 400 * flops)(
        odd_basis, window
    )
    odd_previous = odd_up(rounded_upper)
    even_upper, rounded_upper = call(functools.partial(upper_products_kernel, False, base), products_outs, 0)(
        message, window
    )
    even_previous = even_up(rounded_upper)
    left, right, factors = call(
        factors_kernel,
        (
            whole(bf16, mats, row_count, 8 * rank),
            whole(bf16, mats, 6 * rank, columns),
            whole(f32, mats, 1, rank, columns),
        ),
        flops // 4,
        out_specs=(IN_VMEM, IN_VMEM, pl.BlockSpec(memory_space=pl.ANY)),
        scratch_shapes=[pltpu.VMEM((mats, 1, rank, columns), f32), pltpu.SemaphoreType.DMA],
    )(message, odd_upper, even_upper, lower_basis, lower_products)
    updated = call(
        update_kernel,
        whole(bf16, mats, 1, row_count, columns),
        4 * flops,
        out_specs=pl.BlockSpec(memory_space=pl.ANY),
        scratch_shapes=[pltpu.VMEM((mats, row_count, columns), bf16), pltpu.SemaphoreType.DMA((mats * (-(-columns // (2 * LANES))),))],
    )(left, right, odd_previous, even_previous, window)
    return (updated, factors)


def solution(mesh):
    placed = (P(None, "replica", None, "tensor"), P(None, "replica", None, "tensor"))
    return jax.shard_map(
        shards,
        mesh=mesh,
        in_specs=placed,
        out_specs=(P(None, "replica", None, "tensor"), P(None, "replica", None, "tensor")),
        check_vma=False,
    )
```
